32 devices in a mesh: sec: 2 (over x), sx: 2 (over y), sy: 8 (over z, core).
Axes of the slice: x: 2, y: 2, z: 4, core: 2. Of those that a mesh axis runs over, the one named last changes fastest.
Arguments:
- replay: bfloat16 [2, 8, 32, 2, 8, 256], P('sec', 'sx', 'sy'), may hold values from -6 to 6
- replay_pick: int32 [2, 8, 32], P('sec', 'sx', 'sy'), may hold values from 0 to 1
- w_in: bfloat16 [256, 512], replicated, may hold values from -0.375 to 0.375
- b_in: float32 [512], replicated, may hold values from -3 to 3
- w_out: bfloat16 [512, 8], replicated, may hold values from -0.25 to 0.25
- b_out: float32 [8], replicated, may hold values from -3 to 3
- block_rows: float32 [2, 8, 32, 64, 256], P('sec', 'sx', 'sy'), may hold values from -1.1 to 9.1
- loads: bfloat16 [2, 8, 32, 64, 128], P('sec', 'sx', 'sy'), may hold values from -36 to 36
- fixed_mask: int32 [2, 8, 32, 64], P('sec', 'sx', 'sy'), may hold values 0 or 1
- elem_map: int32 [2, 8, 32], P('sec', 'sx', 'sy'), may hold values from 0 to 31, each once within a row
- cotangent: bfloat16 [2, 8, 32, 64, 128], P('sec', 'sx', 'sy'), may hold values from -0.029907227 to 0.029907227
Outputs:
- solution: float32 [2, 8, 32, 64, 128], P('sec', 'sx', 'sy')
- w_in_grad: float32 [256, 512], replicated
- b_in_grad: float32 [512], replicated
- w_out_grad: float32 [512, 8], replicated
- b_out_grad: float32 [8], replicated
The draws below stay inside these ranges and needn't reach their ends.
Inputs may be any that keep to these rules, and one draw needn't show every extreme that they name: Each row elem_map[s, x, :] is a permutation of 0 to 31.
All inputs are finite; a program needn't handle non-finite values. No bound on the sum of `fixed_mask` on one device may be relied on, other than what follows from the above.
Results may differ from the reference program's by a relative error of at most 0.0047.
Values sent between devices are 32-bit elements; how exact they have to be, the bound alone decides.
A program may use at most 64 MiB of HBM per device.

```python
import jax
import jax.numpy as jnp
from jax import lax

DOF = 64
ELEM = 8
ECOEF = 8
FEAT = 256
HID = 512
REPLAY = 2
LOADS = 128
SWEEPS = 4
SECTIONS = 2
GX = 8
GY = 32
N_SEC = 2


def draw_block_rows(key, part):
    first, second = jax.random.split(jax.random.fold_in(key, 11))
    shape = (SECTIONS, GX, GY, DOF, 4 * DOF)
    noise = jnp.clip(jax.random.normal(first, shape, jnp.float32), -5.0, 5.0)
    pivots = 4.0 + 4.0 * jax.random.uniform(second, (SECTIONS, GX, GY, DOF, 1), jnp.float32)
    row_ids = lax.broadcasted_iota(jnp.int32, (DOF, 4 * DOF), 0)
    col_ids = lax.broadcasted_iota(jnp.int32, (DOF, 4 * DOF), 1)
    block_ids = col_ids // DOF
    on_diag = row_ids == col_ids % DOF
    spread = jnp.where(block_ids == 0, 0.22, jnp.where(block_ids == 3, 0.005, 0.15)).astype(jnp.float32)
    diag_first = jnp.where(on_diag & (block_ids == 0), 1.0, 0.0).astype(jnp.float32)
    diag_last = jnp.where(on_diag & (block_ids == 3), 1.0, 0.0).astype(jnp.float32)
    values = spread * noise + diag_first * pivots + diag_last / pivots
    return values.astype(jnp.float32)


def plant(values, rng, low, top_value):
    longest = values.shape.index(max(values.shape))
    spots = []
    for shift in (0, 1):
        where = [jax.random.randint(jax.random.fold_in(rng, axis), (), 0, length) for axis, length in enumerate(values.shape)]
        where[longest] = (where[longest] + shift) % values.shape[longest]
        spots.append(tuple(where))
    return values.at[spots[0]].set(low).at[spots[1]].set(top_value)


def steps_of(own_key, shape, cuts, smallest, largest):
    level, own = 1.0, jax.random.fold_in(own_key, 6)
    for dim, blocks in cuts:
        heights = jnp.exp(jax.random.uniform(jax.random.fold_in(own, dim), (blocks,), jnp.float32, smallest / len(cuts), largest / len(cuts)))
        level = level * jnp.repeat(heights, shape[dim] // blocks).reshape([-1 if axis == dim else 1 for axis in range(len(shape))])
    return level


def normal_values(own_key, extent, deviation, most, cuts=(), held_as=jnp.bfloat16):
    entries = deviation * jax.random.normal(own_key, extent, jnp.float32)
    if cuts:
        entries = entries * steps_of(own_key, extent, cuts, -0.22, 0.18)
    return jnp.clip(entries, -most, most).astype(held_as)


def setup_inputs(seed: int = 0) -> dict:
    streams_of = jax.random.split(jax.random.key(seed), 12)
    replay = normal_values(streams_of[0], (SECTIONS, GX, GY, REPLAY, ELEM, FEAT), 1.0, 6.0, ((0, 2), (1, 2), (2, 8)))
    replay_pick = plant(jax.random.randint(streams_of[1], (SECTIONS, GX, GY), 0, REPLAY), jax.random.fold_in(streams_of[1], 1), 0, REPLAY - 1).astype(jnp.int32)
    w_in = normal_values(streams_of[2], (FEAT, HID), FEAT ** -0.5, 0.375)
    b_in = normal_values(streams_of[3], (HID,), 0.5, 3.0, (), jnp.float32)
    w_out = normal_values(streams_of[4], (HID, ECOEF), HID ** -0.5, 0.25)
    b_out = normal_values(streams_of[5], (ECOEF,), 0.5, 3.0, (), jnp.float32)
    block_rows = draw_block_rows(jax.random.fold_in(streams_of[11], 71), 0)
    loads = normal_values(streams_of[7], (SECTIONS, GX, GY, DOF, LOADS), 6.0, 36.0, ((0, 2), (1, 2), (2, 8)))
    fixed_mask = plant((jax.random.randint(streams_of[8], (SECTIONS, GX, GY, DOF), 0, 8) < 7).astype(jnp.int32), jax.random.fold_in(streams_of[8], 1), 0, 1)
    elem_map = jax.vmap(lambda own: jax.random.permutation(own, GY))(jax.random.split(streams_of[9], SECTIONS * GX)).reshape((SECTIONS, GX, GY)).astype(jnp.int32)
    cotangent = normal_values(streams_of[10], (SECTIONS, GX, GY, DOF, LOADS), 0.005, 0.029907227, ((0, 2), (1, 2), (2, 8)))
    return {"replay": replay, "replay_pick": replay_pick, "w_in": w_in, "b_in": b_in, "w_out": w_out, "b_out": b_out, "block_rows": block_rows, "loads": loads, "fixed_mask": fixed_mask, "elem_map": elem_map, "cotangent": cotangent}


RELAXATION = 0.8
PRECISE = lax.Precision.HIGHEST


def block_mul(blocks, values):
    return jnp.einsum("xyij,xyjr->xyir", blocks, values, precision=PRECISE)


def block_tmul(blocks, values):
    return jnp.einsum("xyji,xyjr->xyir", blocks, values, precision=PRECISE)


def pick_states(replay, replay_pick):
    chosen = replay[:, :, :, 0]
    for slot_index in range(1, replay.shape[3]):
        chosen = jnp.where((replay_pick == slot_index)[..., None, None], replay[:, :, :, slot_index], chosen)
    return chosen


def network_forward(picked, w_in, b_in, w_out, b_out):
    pre_in = jnp.dot(picked, w_in, preferred_element_type=jnp.float32) + b_in
    hidden = jax.nn.silu(pre_in).astype(jnp.bfloat16)
    pre_out = jnp.dot(hidden, w_out, preferred_element_type=jnp.float32) + b_out
    gate_out = jax.nn.sigmoid(pre_out)
    return pre_in, hidden, gate_out, 0.5 + 2.0 * gate_out


def network_backward(picked, w_out, pre_in, hidden, gate_out, coef_grad):
    out_term = coef_grad * (2.0 * gate_out * (1.0 - gate_out))
    out_round = out_term.astype(jnp.bfloat16)
    w_out_grad = jnp.dot(hidden.T, out_round, preferred_element_type=jnp.float32)
    b_out_grad = jnp.sum(out_term, axis=0)
    back_hidden = jnp.dot(out_round, w_out.T, preferred_element_type=jnp.float32)
    gate_in = jax.nn.sigmoid(pre_in)
    in_term = back_hidden * (gate_in + pre_in * gate_in * (1.0 - gate_in))
    in_round = in_term.astype(jnp.bfloat16)
    w_in_grad = jnp.dot(picked.T, in_round, preferred_element_type=jnp.float32)
    b_in_grad = jnp.sum(in_term, axis=0)
    return w_in_grad, b_in_grad, w_out_grad, b_out_grad


def couple(scene_rows, values):
    east_k = scene_rows[..., DOF:2 * DOF]
    north_k = scene_rows[..., 2 * DOF:3 * DOF]
    zero_col = jnp.zeros_like(values[:, :1])
    zero_row = jnp.zeros_like(values[:1])
    from_east = jnp.concatenate([values[:, 1:], zero_col], axis=1)
    from_north = jnp.concatenate([values[1:], zero_row], axis=0)
    back_east = block_tmul(east_k, values)
    back_north = block_tmul(north_k, values)
    from_west = jnp.concatenate([zero_col, back_east[:, :-1]], axis=1)
    from_south = jnp.concatenate([zero_row, back_north[:-1]], axis=0)
    return block_mul(east_k, from_east) + block_mul(north_k, from_north) + from_west + from_south


def solve_scene(scene_rows, scene_loads, scene_mask, coef_block, scene_cot):
    load_field = scene_loads.astype(jnp.float32)
    keep_mask = scene_mask.astype(jnp.float32)[..., None]
    coef_wide = coef_block[..., None]
    diag_k = scene_rows[..., 0:DOF]
    precond = scene_rows[..., 3 * DOF:4 * DOF]
    field_now = jnp.zeros_like(load_field)
    history = []
    for sweep_index in range(SWEEPS):
        history.append(field_now)
        diag_term = block_mul(diag_k, field_now)
        scaled_res = (load_field - (coef_wide * diag_term + couple(scene_rows, field_now))) / coef_wide
        field_now = keep_mask * (field_now + RELAXATION * block_mul(precond, scaled_res))
    grad_field = scene_cot.astype(jnp.float32)
    coef_grad = jnp.zeros_like(coef_block)
    for sweep_index in reversed(range(SWEEPS)):
        prior = history[sweep_index]
        diag_term = block_mul(diag_k, prior)
        scaled_res = (load_field - (coef_wide * diag_term + couple(scene_rows, prior))) / coef_wide
        masked_grad = keep_mask * grad_field
        pushed = RELAXATION * block_tmul(precond, masked_grad)
        scaled_grad = pushed / coef_wide
        coef_grad = coef_grad - jnp.sum(scaled_grad * (scaled_res + diag_term), axis=-1)
        if sweep_index > 0:
            grad_field = masked_grad - (block_tmul(diag_k, coef_wide * scaled_grad) + couple(scene_rows, scaled_grad))
    return field_now, coef_grad


def reference(replay, replay_pick, w_in, b_in, w_out, b_out, block_rows, loads, fixed_mask, elem_map, cotangent):
    picked = pick_states(replay, replay_pick).reshape(-1, FEAT)
    pre_in, hidden, gate_out, coef_rows = network_forward(picked, w_in, b_in, w_out, b_out)
    groups = coef_rows.reshape(N_SEC, GX, GY, DOF)
    row_index = jnp.arange(GX).astype(jnp.int32)[:, None]
    solutions = []
    returned = [None] * N_SEC
    for scene_index in range(N_SEC):
        other = N_SEC - 1 - scene_index
        column_index = elem_map[scene_index].astype(jnp.int32)
        coef_block = groups[other][row_index, column_index]
        field_now, coef_grad = solve_scene(block_rows[scene_index], loads[scene_index], fixed_mask[scene_index], coef_block, cotangent[scene_index])
        solutions.append(field_now)
        returned[other] = jnp.zeros((GX, GY, DOF), jnp.float32).at[row_index, column_index].set(coef_grad)
    group_grad = jnp.stack(returned, axis=0).reshape(-1, ECOEF)
    w_in_grad, b_in_grad, w_out_grad, b_out_grad = network_backward(picked, w_out, pre_in, hidden, gate_out, group_grad)
    return (jnp.stack(solutions, axis=0), w_in_grad, b_in_grad, w_out_grad, b_out_grad)
```

```python
import functools

import jax
import jax.numpy as jnp
from jax import lax
from jax.experimental import pallas as pl
from jax.experimental.pallas import tpu as pltpu
from jax.sharding import PartitionSpec as P

SWEEPS = 4
RELAXATION = 0.8
F32 = jnp.float32
BF16 = jnp.bfloat16
MESH = pl.DeviceIdType.MESH


def mm(a, b):
    return jnp.dot(a, b, preferred_element_type=F32)


def mm_nt(a, b):
    return lax.dot_general(a, b, (((1,), (1,)), ((), ())), preferred_element_type=F32)


def split(v):
    hi = v.astype(BF16)
    lo = (v - hi.astype(F32)).astype(BF16)
    return hi, lo


def mul3(m3, v):
    hi, lo = split(v)
    return mm(m3, jnp.concatenate([hi, hi, lo], axis=0))


def put3(ref, bx, by, m):
    d = m.shape[0]
    hi, lo = split(m)
    ref[bx, by, :, 0:d] = hi
    ref[bx, by, :, d : 2 * d] = lo
    ref[bx, by, :, 2 * d : 3 * d] = hi


def kernel(
    n_sx, n_sy, picked_ref, w_in_ref, b_in_ref, wt_ref, b_out_ref, rows_ref, loads_ref, mask_ref, map_ref,
    cot_ref, u_ref, wg_ref, ex_ref,
    pre, hid, pick_t, gate, own, gath, placed, back, oh, kh_w, kh_s, cm, kd3, kdt3, p3, pt3, mw, cw, rc,
    x_st, h_w, h_e, h_s, h_n, xb, tt, ku, gh, acc_hi, acc_lo,
    sg, rg, sk, rk, s_we, r_we, s_ns, r_ns, sc, rcs,
):
    bx, by, dof = rows_ref.shape[0], rows_ref.shape[1], rows_ref.shape[2]
    groups = bx * by
    lanes = loads_ref.shape[3]
    sec, sx, sy = lax.axis_index("sec"), lax.axis_index("sx"), lax.axis_index("sy")
    has_w, has_e, has_s, has_n = sy > 0, sy < n_sy - 1, sx > 0, sx < n_sx - 1
    west, east = (sec, sx, sy - 1), (sec, sx, sy + 1)
    south, north = (sec, sx - 1, sy), (sec, sx + 1, sy)

    barrier = pltpu.get_barrier_semaphore()
    for k in range(n_sy):
        pl.semaphore_signal(
            barrier, inc=1, device_id=(1 - sec, sx, lax.rem(sy + k, n_sy)), device_id_type=MESH
        )
    for has, dev in ((has_w, west), (has_e, east), (has_s, south), (has_n, north)):

        @pl.when(has)
        def _():
            pl.semaphore_signal(barrier, inc=1, device_id=dev, device_id_type=MESH)

    pre_in = mm(picked_ref[...], w_in_ref[...]) + b_in_ref[...]
    pre[...] = pre_in
    hidden = (pre_in * jax.nn.sigmoid(pre_in)).astype(BF16)
    hid[...] = hidden
    n_rows = hidden.shape[0]
    full = jax.nn.sigmoid(mm_nt(hidden, wt_ref[...]) + b_out_ref[...])
    elem = n_rows // groups
    width = dof // elem
    wide = full.shape[1]
    row_id = lax.broadcasted_iota(jnp.int32, (n_rows, wide), 0)
    col_id = lax.broadcasted_iota(jnp.int32, (n_rows, wide), 1)
    mine = (row_id % elem) == (col_id // width)
    gate_rows = jnp.sum(jnp.where(mine, full, 0.0).reshape(groups, elem, wide), axis=1)
    gate[...] = gate_rows
    own[...] = 0.5 + 2.0 * gate_rows

    one = lambda has: jnp.where(has, 1, 0)
    pl.semaphore_wait(barrier, n_sy + one(has_w) + one(has_e) + one(has_s) + one(has_n))

    def group_copy(k):
        j = lax.rem(sy + k, n_sy)
        return pltpu.make_async_remote_copy(
            src_ref=own, dst_ref=gath.at[sy], send_sem=sg.at[k], recv_sem=rg.at[sy],
            device_id=(1 - sec, sx, j), device_id_type=MESH,
        )

    for k in range(n_sy):
        group_copy(k).start()

    def kw_copy():
        return pltpu.make_async_remote_copy(
            src_ref=rows_ref.at[:, by - 1, :, pl.ds(0, 2 * dof)], dst_ref=kh_w,
            send_sem=sk.at[0], recv_sem=rk.at[0], device_id=east, device_id_type=MESH,
        )

    def ks_copy():
        return pltpu.make_async_remote_copy(
            src_ref=rows_ref.at[bx - 1, :, :, pl.ds(2 * dof, 2 * dof)], dst_ref=kh_s,
            send_sem=sk.at[1], recv_sem=rk.at[1], device_id=north, device_id_type=MESH,
        )

    @pl.when(has_e)
    def _():
        kw_copy().start()

    @pl.when(has_n)
    def _():
        ks_copy().start()

    zero_block = jnp.zeros((dof, dof), BF16)
    for x in range(bx):
        for y in range(by):
            block = rows_ref[x, y]
            turned = block.T
            cm[x, y, :, 0 : 2 * dof] = block[:, dof : 3 * dof].astype(BF16)
            put3(kd3, x, y, block[:, 0:dof])
            put3(p3, x, y, block[:, 3 * dof : 4 * dof])
            put3(kdt3, x, y, turned[0:dof])
            put3(pt3, x, y, turned[3 * dof : 4 * dof])
            if y + 1 < by:
                cm[x, y + 1, :, 2 * dof : 3 * dof] = turned[dof : 2 * dof].astype(BF16)
            if x + 1 < bx:
                cm[x + 1, y, :, 3 * dof : 4 * dof] = turned[2 * dof : 3 * dof].astype(BF16)
            mw[x, y] = jnp.broadcast_to(mask_ref[:, x * by + y : x * by + y + 1], (dof, lanes))
    pick_t[...] = picked_ref[...].astype(F32).T.astype(BF16)
    xb[...] = jnp.zeros_like(xb)

    span = n_sy * groups
    ids = lax.broadcasted_iota(jnp.int32, (span, lanes), 0)
    gid = (ids // groups) * by + ids % by
    gx = (ids // by) % bx
    for x in range(bx):
        for y in range(by):
            b = x * by + y
            hit = (gid == map_ref[x, y]) & (gx == x)
            oh[:, b * lanes : (b + 1) * lanes] = jnp.where(hit, 1.0, 0.0).astype(BF16)

    for j in range(n_sy):
        pltpu.make_async_remote_copy(
            src_ref=own, dst_ref=gath.at[j], send_sem=sg.at[j], recv_sem=rg.at[j],
            device_id=(1 - sec, sx, j), device_id_type=MESH,
        ).wait_recv()
    turned_rows = gath[...].reshape(span, wide).T[0:dof]
    g_hi, g_lo = split(turned_rows)
    for x in range(bx):
        part = oh[:, x * by * lanes : (x + 1) * by * lanes]
        coefs = mm(g_hi, part) + mm(g_lo, part)
        for y in range(by):
            c = coefs[:, y * lanes : (y + 1) * lanes]
            rc[x, y] = 1.0 / c

    def face(direction, r, x):
        if direction == 0:
            return pltpu.make_async_remote_copy(
                src_ref=x_st.at[r, x, 0], dst_ref=h_e.at[r, x], send_sem=s_we.at[0, r, x],
                recv_sem=r_we.at[0, r, x], device_id=west, device_id_type=MESH,
            )
        if direction == 1:
            return pltpu.make_async_remote_copy(
                src_ref=x_st.at[r, x, by - 1], dst_ref=h_w.at[r, x], send_sem=s_we.at[1, r, x],
                recv_sem=r_we.at[1, r, x], device_id=east, device_id_type=MESH,
            )
        if direction == 2:
            return pltpu.make_async_remote_copy(
                src_ref=x_st.at[r, 0], dst_ref=h_n.at[r], send_sem=s_ns.at[0, r],
                recv_sem=r_ns.at[0, r], device_id=south, device_id_type=MESH,
            )
        return pltpu.make_async_remote_copy(
            src_ref=x_st.at[r, bx - 1], dst_ref=h_s.at[r], send_sem=s_ns.at[1, r],
            recv_sem=r_ns.at[1, r], device_id=north, device_id_type=MESH,
        )

    def send_row(r, x):
        @pl.when((r < SWEEPS - 1) & (x == bx - 1) & has_n)
        def _():
            face(3, r, x).start()

        @pl.when((r < SWEEPS - 1) & (x == 0) & has_s)
        def _():
            face(2, r, x).start()

        @pl.when((r < SWEEPS - 1) & has_w)
        def _():
            face(0, r, x).start()

        @pl.when((r < SWEEPS - 1) & has_e)
        def _():
            face(1, r, x).start()

    def row_at(k):
        return jnp.where(sx == 0, k, bx - 1 - k)

    def finish(r, x, y, u, h):
        m = mw[x, y]
        p = RELAXATION * mul3(pt3[x, y], h)
        w = p * rc[x, y]
        x_st[r, x, y, :, 0:lanes] = u
        x_st[r, x, y, :, lanes : 2 * lanes] = w
        slot = lax.rem(r, 2)
        xb[slot, x + 1, y + 1, :, 0:lanes] = u.astype(BF16)
        xb[slot, x + 1, y + 1, :, lanes : 2 * lanes] = w.astype(BF16)
        u_ref[x, y] = u
        gh[x, y] = h
        cw[x, y] = p

    def after(x):
        for y in range(by):
            gh[x, y] = gh[x, y] - mul3(kdt3[x, y], cw[x, y])
            ku[x, y] = mul3(kd3[x, y], u_ref[x, y])

    def first_row(k, _):
        x = row_at(k)
        for y in range(by):
            t = loads_ref[x, y].astype(F32) * rc[x, y]
            tt[0, x, y] = t
            u = mw[x, y] * (RELAXATION * mul3(p3[x, y], t))
            finish(0, x, y, u, mw[x, y] * cot_ref[x, y].astype(F32))
        send_row(0, x)
        after(x)
        return 0

    lax.fori_loop(0, bx, first_row, 0)

    @pl.when(has_w)
    def _():
        kw_copy().wait_recv()
        for x in range(bx):
            cm[x, 0, :, 2 * dof : 3 * dof] = kh_w[x].T[dof : 2 * dof].astype(BF16)

    @pl.when(jnp.logical_not(has_w))
    def _():
        for x in range(bx):
            cm[x, 0, :, 2 * dof : 3 * dof] = zero_block

    @pl.when(has_s)
    def _():
        ks_copy().wait_recv()
        for y in range(by):
            cm[0, y, :, 3 * dof : 4 * dof] = kh_s[y].T[0:dof].astype(BF16)

    @pl.when(jnp.logical_not(has_s))
    def _():
        for y in range(by):
            cm[0, y, :, 3 * dof : 4 * dof] = zero_block

    def sweep(r, _):
        old = lax.rem(r - 1, 2)

        def sweep_row(k, _):
            x = row_at(k)

            @pl.when(has_w)
            def _():
                face(1, r - 1, x).wait_recv()
                xb[old, x + 1, 0] = h_w[r - 1, x].astype(BF16)

            @pl.when(has_e)
            def _():
                face(0, r - 1, x).wait_recv()
                xb[old, x + 1, by + 1] = h_e[r - 1, x].astype(BF16)

            @pl.when((x == 0) & has_s)
            def _():
                face(3, r - 1, x).wait_recv()
                for y in range(by):
                    xb[old, 0, y + 1] = h_s[r - 1, y].astype(BF16)

            @pl.when((x == bx - 1) & has_n)
            def _():
                face(2, r - 1, x).wait_recv()
                for y in range(by):
                    xb[old, bx + 1, y + 1] = h_n[r - 1, y].astype(BF16)

            for y in range(by):
                near = jnp.concatenate(
                    [xb[old, x + 1, y + 2], xb[old, x + 2, y + 1], xb[old, x + 1, y], xb[old, x, y + 1]],
                    axis=0,
                )
                c = mm(cm[x, y], near)
                t = (loads_ref[x, y].astype(F32) - c[:, 0:lanes]) * rc[x, y]
                tt[r, x, y] = t
                m = mw[x, y]
                u = m * (u_ref[x, y] + RELAXATION * mul3(p3[x, y], t - ku[x, y]))
                finish(r, x, y, u, m * (gh[x, y] - c[:, lanes : 2 * lanes]))
            send_row(r, x)

            @pl.when(r < SWEEPS - 1)
            def _():
                after(x)

            return 0

        return lax.fori_loop(0, bx, sweep_row, 0)

    lax.fori_loop(1, SWEEPS, sweep, 0)

    for x in range(bx):
        for y in range(by):
            total = tt[0, x, y] * x_st[SWEEPS - 1, x, y, :, lanes : 2 * lanes]
            for r in range(1, SWEEPS):
                total = total + tt[r, x, y] * x_st[SWEEPS - 1 - r, x, y, :, lanes : 2 * lanes]
            hi, lo = split(-total)
            b = x * by + y
            acc_hi[:, b * lanes : (b + 1) * lanes] = hi
            acc_lo[:, b * lanes : (b + 1) * lanes] = lo
    sums = mm_nt(oh[...], acc_hi[...]) + mm_nt(oh[...], acc_lo[...])
    sums = jnp.concatenate([sums, jnp.zeros((span, wide - dof), F32)], axis=1)
    placed[...] = sums.reshape(n_sy, groups, wide)

    def grad_copy(k):
        j = lax.rem(sy + k, n_sy)
        return pltpu.make_async_remote_copy(
            src_ref=placed.at[j], dst_ref=back.at[sy], send_sem=sc.at[k], recv_sem=rcs.at[sy],
            device_id=(1 - sec, sx, j), device_id_type=MESH,
        )

    for k in range(n_sy):
        grad_copy(k).start()

    pre_in = pre[...]
    q = jax.nn.sigmoid(pre_in)
    slope = q + pre_in * q * (1.0 - q)

    for j in range(n_sy):
        pltpu.make_async_remote_copy(
            src_ref=placed.at[j], dst_ref=back.at[j], send_sem=sc.at[j], recv_sem=rcs.at[j],
            device_id=(1 - sec, sx, j), device_id_type=MESH,
        ).wait_recv()
    net_grad = jnp.sum(back[...], axis=0)
    g = gate[...]
    out_term = net_grad * (2.0 * g * (1.0 - g))
    spread = jnp.broadcast_to(out_term[:, None, :], (groups, elem, wide)).reshape(n_rows, wide)
    spread = jnp.where(mine, spread, 0.0)
    out_round = spread.astype(BF16)
    turned_out = spread.T.astype(BF16)
    w_out_t = mm(turned_out, hid[...])[0:dof]
    hidden_units = w_out_t.shape[1]
    ex_ref[0:width] = jnp.sum(w_out_t.reshape(elem, width, hidden_units), axis=0)
    in_term = mm(out_round, wt_ref[...]) * slope
    wg_ref[...] = mm(pick_t[...], in_term.astype(BF16))
    tail = jnp.concatenate(
        [
            jnp.sum(in_term, axis=0, keepdims=True),
            jnp.concatenate(
                [jnp.sum(out_term, axis=0, keepdims=True), jnp.zeros((1, hidden_units - wide), F32)], axis=1
            ),
            jnp.zeros((6, hidden_units), F32),
        ],
        axis=0,
    )
    ex_ref[width : width + 8] = tail

    for k in range(n_sy):
        group_copy(k).wait_send()
        grad_copy(k).wait_send()

    @pl.when(has_e)
    def _():
        kw_copy().wait_send()

    @pl.when(has_n)
    def _():
        ks_copy().wait_send()

    for r in range(SWEEPS - 1):
        for x in range(bx):

            @pl.when(has_w)
            def _():
                face(0, r, x).wait_send()

            @pl.when(has_e)
            def _():
                face(1, r, x).wait_send()

        @pl.when(has_s)
        def _():
            face(2, r, 0).wait_send()

        @pl.when(has_n)
        def _():
            face(3, r, 0).wait_send()


def local(
    replay, replay_pick, w_in, b_in, w_out, b_out, block_rows, loads, fixed_mask, elem_map, cotangent
):
    _, bx, by, dof, _ = block_rows.shape
    lanes = loads.shape[-1]
    n_sx, n_sy = lax.axis_size("sx"), lax.axis_size("sy")
    feat, hidden_units = w_in.shape
    ecoef = w_out.shape[1]
    groups = bx * by
    wide = 2 * dof
    picked = replay[:, :, :, 0]
    picked = jnp.where((replay_pick == 1)[..., None, None], replay[:, :, :, 1], picked)
    picked = picked.reshape(-1, feat)
    n_rows = picked.shape[0]
    elem = n_rows // groups
    wt = jnp.concatenate([jnp.tile(w_out.T, (elem, 1)), jnp.zeros((wide - dof, hidden_units), BF16)], axis=0)
    bt = jnp.concatenate([jnp.tile(b_out, elem), jnp.zeros((wide - dof,), F32)])[None]
    mask = fixed_mask.reshape(groups, dof).T.astype(F32)
    vm = lambda: pl.BlockSpec(memory_space=pltpu.VMEM)
    sm = lambda: pl.BlockSpec(memory_space=pltpu.SMEM)
    dma = pltpu.SemaphoreType.DMA
    rounds = SWEEPS - 1
    span = n_sy * groups
    scratch = [
        pltpu.VMEM((n_rows, hidden_units), F32),
        pltpu.VMEM((n_rows, hidden_units), BF16),
        pltpu.VMEM((feat, n_rows), BF16),
        pltpu.VMEM((groups, wide), F32),
        pltpu.VMEM((groups, wide), F32),
        pltpu.VMEM((n_sy, groups, wide), F32),
        pltpu.VMEM((n_sy, groups, wide), F32),
        pltpu.VMEM((n_sy, groups, wide), F32),
        pltpu.VMEM((span, groups * lanes), BF16),
        pltpu.VMEM((bx, dof, 2 * dof), F32),
        pltpu.VMEM((by, dof, 2 * dof), F32),
        pltpu.VMEM((bx, by, dof, 4 * dof), BF16),
        pltpu.VMEM((bx, by, dof, 3 * dof), BF16),
        pltpu.VMEM((bx, by, dof, 3 * dof), BF16),
        pltpu.VMEM((bx, by, dof, 3 * dof), BF16),
        pltpu.VMEM((bx, by, dof, 3 * dof), BF16),
        pltpu.VMEM((bx, by, dof, lanes), F32),
        pltpu.VMEM((bx, by, dof, lanes), F32),
        pltpu.VMEM((bx, by, dof, lanes), F32),
        pltpu.VMEM((SWEEPS, bx, by, dof, 2 * lanes), F32),
        pltpu.VMEM((rounds, bx, dof, 2 * lanes), F32),
        pltpu.VMEM((rounds, bx, dof, 2 * lanes), F32),
        pltpu.VMEM((rounds, by, dof, 2 * lanes), F32),
        pltpu.VMEM((rounds, by, dof, 2 * lanes), F32),
        pltpu.VMEM((2, bx + 2, by + 2, dof, 2 * lanes), BF16),
        pltpu.VMEM((SWEEPS, bx, by, dof, lanes), F32),
        pltpu.VMEM((bx, by, dof, lanes), F32),
        pltpu.VMEM((bx, by, dof, lanes), F32),
        pltpu.VMEM((dof, groups * lanes), BF16),
        pltpu.VMEM((dof, groups * lanes), BF16),
        dma((n_sy,)), dma((n_sy,)), dma((2,)), dma((2,)),
        dma((2, rounds, bx)), dma((2, rounds, bx)), dma((2, rounds)), dma((2, rounds)),
        dma((n_sy,)), dma((n_sy,)),
    ]
    field, wg, ex = pl.pallas_call(
        functools.partial(kernel, n_sx, n_sy),
        out_shape=(
            jax.ShapeDtypeStruct((bx, by, dof, lanes), F32),
            jax.ShapeDtypeStruct((feat, hidden_units), F32),
            jax.ShapeDtypeStruct((ecoef + 8, hidden_units), F32),
        ),
        in_specs=[vm()] * 8 + [sm(), vm()],
        out_specs=(vm(), vm(), vm()),
        scratch_shapes=scratch,
        compiler_params=pltpu.CompilerParams(
            collective_id=0, has_side_effects=True, vmem_limit_bytes=48 * 1024 * 1024
        ),
    )(picked, w_in, b_in[None], wt, bt, block_rows[0], loads[0], mask, elem_map[0], cotangent[0])
    wg, ex = lax.psum((wg, ex), ("sec", "sx", "sy"))
    w_out_grad = ex[0:ecoef].T
    b_in_grad = ex[ecoef]
    b_out_grad = jnp.sum(ex[ecoef + 1, 0:dof].reshape(elem, ecoef), axis=0)
    return (field[None], wg, b_in_grad, w_out_grad, b_out_grad)


def solution(mesh):
    placed = (
        P("sec", "sx", "sy", None, None, None),
        P("sec", "sx", "sy"),
        P(),
        P(),
        P(),
        P(),
        P("sec", "sx", "sy", None, None),
        P("sec", "sx", "sy", None, None),
        P("sec", "sx", "sy", None),
        P("sec", "sx", "sy"),
        P("sec", "sx", "sy", None, None),
    )
    return jax.shard_map(
        local,
        mesh=mesh,
        in_specs=placed,
        out_specs=(P("sec", "sx", "sy", None, None), P(), P(), P(), P()),
        check_vma=False,
    )
```

```python
import functools

import jax
import jax.numpy as jnp
from jax import lax
from jax.experimental import pallas as pl
from jax.experimental.pallas import tpu as pltpu
from jax.sharding import PartitionSpec as P

SWEEPS = 4
RELAXATION = 0.8
F32 = jnp.float32
BF16 = jnp.bfloat16
MESH = pl.DeviceIdType.MESH


def mm(a, b):
    return jnp.dot(a, b, preferred_element_type=F32)


def mm_nt(a, b):
    return lax.dot_general(a, b, (((1,), (1,)), ((), ())), preferred_element_type=F32)


def split(v):
    hi = v.astype(BF16)
    lo = (v - hi.astype(F32)).astype(BF16)
    return hi, lo


def mul3(m3, v):
    hi, lo = split(v)
    return mm(m3, jnp.concatenate([hi, hi, lo], axis=0))


def put3(ref, bx, by, m):
    d = m.shape[0]
    hi, lo = split(m)
    ref[bx, by, :, 0:d] = hi
    ref[bx, by, :, d : 2 * d] = lo
    ref[bx, by, :, 2 * d : 3 * d] = hi


def kernel(
    n_sx, n_sy, picked_ref, w_in_ref, b_in_ref, wt_ref, b_out_ref, rows_ref, loads_ref, mask_ref, map_ref,
    cot_ref, u_ref, wg_ref, bi_ref, wo_ref, bo_ref,
    pre, hid, pick_t, gate, own, gath, placed, back, oh, kh_w, kh_s, cm, kd3, kdt3, p3, pt3, mw, cw, rc,
    x_st, h_w, h_e, h_s, h_n, xb, tt, ku, gh, acc_hi, acc_lo,
    red, half, got_core, got_plane, got_z, summed,
    sg, rg, sk, rk, s_we, r_we, s_ns, r_ns, sc, rcs, s_core, r_core, s_plane, r_plane, s_z, r_z,
):
    bx, by, dof = rows_ref.shape[0], rows_ref.shape[1], rows_ref.shape[2]
    groups = bx * by
    lanes = loads_ref.shape[3]
    sec, sx, sy = lax.axis_index("sec"), lax.axis_index("sx"), lax.axis_index("sy")
    has_w, has_e, has_s, has_n = sy > 0, sy < n_sy - 1, sx > 0, sx < n_sx - 1
    west, east = (sec, sx, sy - 1), (sec, sx, sy + 1)
    south, north = (sec, sx - 1, sy), (sec, sx + 1, sy)

    n_plane, n_z = 2 * n_sx, n_sy // 2
    core, my_z, my_plane = lax.rem(sy, 2), sy // 2, sec * n_sx + sx
    mate = (sec, sx, sy + 1 - 2 * core)
    plane_dev = lambda i: (i // n_sx, lax.rem(i, n_sx), sy)
    z_dev = lambda i: (sec, sx, 2 * i + core)

    barrier = pltpu.get_barrier_semaphore()
    pl.semaphore_signal(barrier, inc=1, device_id=mate, device_id_type=MESH)
    for k in range(1, n_plane):
        pl.semaphore_signal(
            barrier, inc=1, device_id=plane_dev(lax.rem(my_plane + k, n_plane)), device_id_type=MESH
        )
    for k in range(1, n_z):
        pl.semaphore_signal(barrier, inc=1, device_id=z_dev(lax.rem(my_z + k, n_z)), device_id_type=MESH)
    for k in range(n_sy):
        pl.semaphore_signal(
            barrier, inc=1, device_id=(1 - sec, sx, lax.rem(sy + k, n_sy)), device_id_type=MESH
        )
    for has, dev in ((has_w, west), (has_e, east), (has_s, south), (has_n, north)):

        @pl.when(has)
        def _():
            pl.semaphore_signal(barrier, inc=1, device_id=dev, device_id_type=MESH)

    pre_in = mm(picked_ref[...], w_in_ref[...]) + b_in_ref[...]
    pre[...] = pre_in
    hidden = (pre_in * jax.nn.sigmoid(pre_in)).astype(BF16)
    hid[...] = hidden
    n_rows = hidden.shape[0]
    full = jax.nn.sigmoid(mm_nt(hidden, wt_ref[...]) + b_out_ref[...])
    elem = n_rows // groups
    width = dof // elem
    wide = full.shape[1]
    row_id = lax.broadcasted_iota(jnp.int32, (n_rows, wide), 0)
    col_id = lax.broadcasted_iota(jnp.int32, (n_rows, wide), 1)
    mine = (row_id % elem) == (col_id // width)
    gate_rows = jnp.sum(jnp.where(mine, full, 0.0).reshape(groups, elem, wide), axis=1)
    gate[...] = gate_rows
    own[...] = 0.5 + 2.0 * gate_rows

    one = lambda has: jnp.where(has, 1, 0)
    pl.semaphore_wait(barrier, n_sy + n_plane + n_z - 1 + one(has_w) + one(has_e) + one(has_s) + one(has_n))

    def group_copy(k):
        j = lax.rem(sy + k, n_sy)
        return pltpu.make_async_remote_copy(
            src_ref=own, dst_ref=gath.at[sy], send_sem=sg.at[k], recv_sem=rg.at[sy],
            device_id=(1 - sec, sx, j), device_id_type=MESH,
        )

    for k in range(n_sy):
        group_copy(k).start()

    def kw_copy():
        return pltpu.make_async_remote_copy(
            src_ref=rows_ref.at[:, by - 1, :, pl.ds(0, 2 * dof)], dst_ref=kh_w,
            send_sem=sk.at[0], recv_sem=rk.at[0], device_id=east, device_id_type=MESH,
        )

    def ks_copy():
        return pltpu.make_async_remote_copy(
            src_ref=rows_ref.at[bx - 1, :, :, pl.ds(2 * dof, 2 * dof)], dst_ref=kh_s,
            send_sem=sk.at[1], recv_sem=rk.at[1], device_id=north, device_id_type=MESH,
        )

    @pl.when(has_e)
    def _():
        kw_copy().start()

    @pl.when(has_n)
    def _():
        ks_copy().start()

    zero_block = jnp.zeros((dof, dof), BF16)
    for x in range(bx):
        for y in range(by):
            block = rows_ref[x, y]
            turned = block.T
            cm[x, y, :, 0 : 2 * dof] = block[:, dof : 3 * dof].astype(BF16)
            put3(kd3, x, y, block[:, 0:dof])
            put3(p3, x, y, block[:, 3 * dof : 4 * dof])
            put3(kdt3, x, y, turned[0:dof])
            put3(pt3, x, y, turned[3 * dof : 4 * dof])
            if y + 1 < by:
                cm[x, y + 1, :, 2 * dof : 3 * dof] = turned[dof : 2 * dof].astype(BF16)
            if x + 1 < bx:
                cm[x + 1, y, :, 3 * dof : 4 * dof] = turned[2 * dof : 3 * dof].astype(BF16)
            mw[x, y] = jnp.broadcast_to(mask_ref[:, x * by + y : x * by + y + 1], (dof, lanes))
    pick_t[...] = picked_ref[...].astype(F32).T.astype(BF16)
    xb[...] = jnp.zeros_like(xb)

    span = n_sy * groups
    ids = lax.broadcasted_iota(jnp.int32, (span, lanes), 0)
    gid = (ids // groups) * by + ids % by
    gx = (ids // by) % bx
    for x in range(bx):
        for y in range(by):
            b = x * by + y
            hit = (gid == map_ref[x, y]) & (gx == x)
            oh[:, b * lanes : (b + 1) * lanes] = jnp.where(hit, 1.0, 0.0).astype(BF16)

    for j in range(n_sy):
        pltpu.make_async_remote_copy(
            src_ref=own, dst_ref=gath.at[j], send_sem=sg.at[j], recv_sem=rg.at[j],
            device_id=(1 - sec, sx, j), device_id_type=MESH,
        ).wait_recv()
    turned_rows = gath[...].reshape(span, wide).T[0:dof]
    g_hi, g_lo = split(turned_rows)
    for x in range(bx):
        part = oh[:, x * by * lanes : (x + 1) * by * lanes]
        coefs = mm(g_hi, part) + mm(g_lo, part)
        for y in range(by):
            c = coefs[:, y * lanes : (y + 1) * lanes]
            rc[x, y] = 1.0 / c

    def face(direction, r, x):
        if direction == 0:
            return pltpu.make_async_remote_copy(
                src_ref=x_st.at[r, x, 0], dst_ref=h_e.at[r, x], send_sem=s_we.at[0, r, x],
                recv_sem=r_we.at[0, r, x], device_id=west, device_id_type=MESH,
            )
        if direction == 1:
            return pltpu.make_async_remote_copy(
                src_ref=x_st.at[r, x, by - 1], dst_ref=h_w.at[r, x], send_sem=s_we.at[1, r, x],
                recv_sem=r_we.at[1, r, x], device_id=east, device_id_type=MESH,
            )
        if direction == 2:
            return pltpu.make_async_remote_copy(
                src_ref=x_st.at[r, 0], dst_ref=h_n.at[r], send_sem=s_ns.at[0, r],
                recv_sem=r_ns.at[0, r], device_id=south, device_id_type=MESH,
            )
        return pltpu.make_async_remote_copy(
            src_ref=x_st.at[r, bx - 1], dst_ref=h_s.at[r], send_sem=s_ns.at[1, r],
            recv_sem=r_ns.at[1, r], device_id=north, device_id_type=MESH,
        )

    def send_row(r, x):
        @pl.when((r < SWEEPS - 1) & (x == bx - 1) & has_n)
        def _():
            face(3, r, x).start()

        @pl.when((r < SWEEPS - 1) & (x == 0) & has_s)
        def _():
            face(2, r, x).start()

        @pl.when((r < SWEEPS - 1) & has_w)
        def _():
            face(0, r, x).start()

        @pl.when((r < SWEEPS - 1) & has_e)
        def _():
            face(1, r, x).start()

    def row_at(k):
        return jnp.where(sx == 0, k, bx - 1 - k)

    def finish(r, x, y, u, h):
        m = mw[x, y]
        p = RELAXATION * mul3(pt3[x, y], h)
        w = p * rc[x, y]
        x_st[r, x, y, :, 0:lanes] = u
        x_st[r, x, y, :, lanes : 2 * lanes] = w
        slot = lax.rem(r, 2)
        xb[slot, x + 1, y + 1, :, 0:lanes] = u.astype(BF16)
        xb[slot, x + 1, y + 1, :, lanes : 2 * lanes] = w.astype(BF16)
        u_ref[x, y] = u
        gh[x, y] = h
        cw[x, y] = p

    def after(x):
        for y in range(by):
            gh[x, y] = gh[x, y] - mul3(kdt3[x, y], cw[x, y])
            ku[x, y] = mul3(kd3[x, y], u_ref[x, y])

    def first_row(k, _):
        x = row_at(k)
        for y in range(by):
            t = loads_ref[x, y].astype(F32) * rc[x, y]
            tt[0, x, y] = t
            u = mw[x, y] * (RELAXATION * mul3(p3[x, y], t))
            finish(0, x, y, u, mw[x, y] * cot_ref[x, y].astype(F32))
        send_row(0, x)
        after(x)
        return 0

    lax.fori_loop(0, bx, first_row, 0)

    @pl.when(has_w)
    def _():
        kw_copy().wait_recv()
        for x in range(bx):
            cm[x, 0, :, 2 * dof : 3 * dof] = kh_w[x].T[dof : 2 * dof].astype(BF16)

    @pl.when(jnp.logical_not(has_w))
    def _():
        for x in range(bx):
            cm[x, 0, :, 2 * dof : 3 * dof] = zero_block

    @pl.when(has_s)
    def _():
        ks_copy().wait_recv()
        for y in range(by):
            cm[0, y, :, 3 * dof : 4 * dof] = kh_s[y].T[0:dof].astype(BF16)

    @pl.when(jnp.logical_not(has_s))
    def _():
        for y in range(by):
            cm[0, y, :, 3 * dof : 4 * dof] = zero_block

    def sweep(r, _):
        old = lax.rem(r - 1, 2)

        def sweep_row(k, _):
            x = row_at(k)

            @pl.when(has_w)
            def _():
                face(1, r - 1, x).wait_recv()
                xb[old, x + 1, 0] = h_w[r - 1, x].astype(BF16)

            @pl.when(has_e)
            def _():
                face(0, r - 1, x).wait_recv()
                xb[old, x + 1, by + 1] = h_e[r - 1, x].astype(BF16)

            @pl.when((x == 0) & has_s)
            def _():
                face(3, r - 1, x).wait_recv()
                for y in range(by):
                    xb[old, 0, y + 1] = h_s[r - 1, y].astype(BF16)

            @pl.when((x == bx - 1) & has_n)
            def _():
                face(2, r - 1, x).wait_recv()
                for y in range(by):
                    xb[old, bx + 1, y + 1] = h_n[r - 1, y].astype(BF16)

            for y in range(by):
                near = jnp.concatenate(
                    [xb[old, x + 1, y + 2], xb[old, x + 2, y + 1], xb[old, x + 1, y], xb[old, x, y + 1]],
                    axis=0,
                )
                c = mm(cm[x, y], near)
                t = (loads_ref[x, y].astype(F32) - c[:, 0:lanes]) * rc[x, y]
                tt[r, x, y] = t
                m = mw[x, y]
                u = m * (u_ref[x, y] + RELAXATION * mul3(p3[x, y], t - ku[x, y]))
                finish(r, x, y, u, m * (gh[x, y] - c[:, lanes : 2 * lanes]))
            send_row(r, x)

            @pl.when(r < SWEEPS - 1)
            def _():
                after(x)

            return 0

        return lax.fori_loop(0, bx, sweep_row, 0)

    lax.fori_loop(1, SWEEPS, sweep, 0)

    for x in range(bx):
        for y in range(by):
            total = tt[0, x, y] * x_st[SWEEPS - 1, x, y, :, lanes : 2 * lanes]
            for r in range(1, SWEEPS):
                total = total + tt[r, x, y] * x_st[SWEEPS - 1 - r, x, y, :, lanes : 2 * lanes]
            hi, lo = split(-total)
            b = x * by + y
            acc_hi[:, b * lanes : (b + 1) * lanes] = hi
            acc_lo[:, b * lanes : (b + 1) * lanes] = lo
    sums = mm_nt(oh[...], acc_hi[...]) + mm_nt(oh[...], acc_lo[...])
    sums = jnp.concatenate([sums, jnp.zeros((span, wide - dof), F32)], axis=1)
    placed[...] = sums.reshape(n_sy, groups, wide)

    def grad_copy(k):
        j = lax.rem(sy + k, n_sy)
        return pltpu.make_async_remote_copy(
            src_ref=placed.at[j], dst_ref=back.at[sy], send_sem=sc.at[k], recv_sem=rcs.at[sy],
            device_id=(1 - sec, sx, j), device_id_type=MESH,
        )

    for k in range(n_sy):
        grad_copy(k).start()

    pre_in = pre[...]
    q = jax.nn.sigmoid(pre_in)
    slope = q + pre_in * q * (1.0 - q)

    for j in range(n_sy):
        pltpu.make_async_remote_copy(
            src_ref=placed.at[j], dst_ref=back.at[j], send_sem=sc.at[j], recv_sem=rcs.at[j],
            device_id=(1 - sec, sx, j), device_id_type=MESH,
        ).wait_recv()
    net_grad = jnp.sum(back[...], axis=0)
    g = gate[...]
    out_term = net_grad * (2.0 * g * (1.0 - g))
    spread = jnp.broadcast_to(out_term[:, None, :], (groups, elem, wide)).reshape(n_rows, wide)
    spread = jnp.where(mine, spread, 0.0)
    out_round = spread.astype(BF16)
    turned_out = spread.T.astype(BF16)
    w_out_t = mm(turned_out, hid[...])[0:dof]
    hidden_units = w_out_t.shape[1]
    in_term = mm(out_round, wt_ref[...]) * slope
    w_in_grad = mm(pick_t[...], in_term.astype(BF16))
    extra = jnp.concatenate(
        [
            jnp.sum(w_out_t.reshape(elem, width, hidden_units), axis=0),
            jnp.sum(in_term, axis=0, keepdims=True),
            jnp.concatenate(
                [jnp.sum(out_term, axis=0, keepdims=True), jnp.zeros((1, hidden_units - wide), F32)], axis=1
            ),
            jnp.zeros((6, hidden_units), F32),
        ],
        axis=0,
    )

    feat = w_in_grad.shape[0]
    strips, deep, more = hidden_units // 128, feat // 8, extra.shape[0] // 8
    tiles = red.shape[0]
    n_half, per = tiles // 2, got_z.shape[1]
    used = strips * (deep + more)
    for c in range(strips):
        red[c * deep : (c + 1) * deep] = w_in_grad[:, c * 128 : (c + 1) * 128].reshape(deep, 8, 128)
        at = strips * deep + c * more
        red[at : at + more] = extra[:, c * 128 : (c + 1) * 128].reshape(more, 8, 128)
    if used < tiles:
        red[used:tiles] = jnp.zeros((tiles - used, 8, 128), F32)

    def core_copy(step, src, dst):
        return pltpu.make_async_remote_copy(
            src_ref=src, dst_ref=dst, send_sem=s_core.at[step], recv_sem=r_core.at[step],
            device_id=mate, device_id_type=MESH,
        )

    give = core_copy(0, red.at[pl.ds((1 - core) * n_half, n_half)], got_core)
    give.start()
    give.wait_recv()
    half[...] = red[pl.ds(core * n_half, n_half)] + got_core[...]

    def plane_copy(step, k, src, dst, slot):
        return pltpu.make_async_remote_copy(
            src_ref=src, dst_ref=dst, send_sem=s_plane.at[step, k], recv_sem=r_plane.at[step, slot],
            device_id=plane_dev(lax.rem(my_plane + k, n_plane)), device_id_type=MESH,
        )

    def plane_give(k):
        to = lax.rem(my_plane + k, n_plane)
        return plane_copy(0, k, half.at[pl.ds(to * per, per)], got_plane.at[my_plane], my_plane)

    def plane_got(k):
        source = lax.rem(my_plane + k, n_plane)
        return plane_copy(0, k, half.at[pl.ds(0, per)], got_plane.at[source], source)

    for k in range(1, n_plane):
        plane_give(k).start()
    part = half[pl.ds(my_plane * per, per)]
    for k in range(1, n_plane):
        plane_got(k).wait_recv()
        part = part + got_plane[lax.rem(my_plane + k, n_plane)]
    got_z[my_z] = part

    def z_copy(k, slot):
        return pltpu.make_async_remote_copy(
            src_ref=got_z.at[my_z], dst_ref=got_z.at[slot], send_sem=s_z.at[k], recv_sem=r_z.at[slot],
            device_id=z_dev(lax.rem(my_z + k, n_z)), device_id_type=MESH,
        )

    for k in range(1, n_z):
        z_copy(k, my_z).start()
    for k in range(1, n_z):
        z_copy(k, lax.rem(my_z + k, n_z)).wait_recv()
    base = core * n_half
    mine_at = pl.ds(base + my_plane * per, per)
    summed[mine_at] = jnp.sum(got_z[...], axis=0)

    def plane_spread(k):
        return plane_copy(1, k, summed.at[mine_at], summed.at[mine_at], my_plane)

    def plane_fill(k):
        source = lax.rem(my_plane + k, n_plane)
        there = summed.at[pl.ds(base + source * per, per)]
        return plane_copy(1, k, there, there, source)

    for k in range(1, n_plane):
        plane_spread(k).start()
    for k in range(1, n_plane):
        plane_fill(k).wait_recv()
    spread_half = core_copy(1, summed.at[pl.ds(base, n_half)], summed.at[pl.ds(base, n_half)])
    spread_half.start()
    other = summed.at[pl.ds((1 - core) * n_half, n_half)]
    core_copy(1, other, other).wait_recv()

    sums = []
    for c in range(strips):
        wg_ref[:, c * 128 : (c + 1) * 128] = summed[c * deep : (c + 1) * deep].reshape(feat, 128)
        at = strips * deep + c * more
        piece = summed[at : at + more].reshape(8 * more, 128)
        wo_ref[c * 128 : (c + 1) * 128, :] = piece.T[:, 0:width]
        bi_ref[:, c * 128 : (c + 1) * 128] = piece[width : width + 1]
        if c == 0:
            folded = piece[width + 1 : width + 2, 0:width]
            for e in range(1, elem):
                folded = folded + piece[width + 1 : width + 2, e * width : (e + 1) * width]
            bo_ref[...] = folded

    give.wait_send()
    spread_half.wait_send()
    for k in range(1, n_plane):
        plane_give(k).wait_send()
        plane_spread(k).wait_send()
    for k in range(1, n_z):
        z_copy(k, my_z).wait_send()
    for k in range(n_sy):
        group_copy(k).wait_send()
        grad_copy(k).wait_send()

    @pl.when(has_e)
    def _():
        kw_copy().wait_send()

    @pl.when(has_n)
    def _():
        ks_copy().wait_send()

    for r in range(SWEEPS - 1):
        for x in range(bx):

            @pl.when(has_w)
            def _():
                face(0, r, x).wait_send()

            @pl.when(has_e)
            def _():
                face(1, r, x).wait_send()

        @pl.when(has_s)
        def _():
            face(2, r, 0).wait_send()

        @pl.when(has_n)
        def _():
            face(3, r, 0).wait_send()


def local(
    replay, replay_pick, w_in, b_in, w_out, b_out, block_rows, loads, fixed_mask, elem_map, cotangent
):
    _, bx, by, dof, _ = block_rows.shape
    lanes = loads.shape[-1]
    n_sx, n_sy = lax.axis_size("sx"), lax.axis_size("sy")
    feat, hidden_units = w_in.shape
    ecoef = w_out.shape[1]
    groups = bx * by
    wide = 2 * dof
    picked = replay[:, :, :, 0]
    picked = jnp.where((replay_pick == 1)[..., None, None], replay[:, :, :, 1], picked)
    picked = picked.reshape(-1, feat)
    n_rows = picked.shape[0]
    elem = n_rows // groups
    wt = jnp.concatenate([jnp.tile(w_out.T, (elem, 1)), jnp.zeros((wide - dof, hidden_units), BF16)], axis=0)
    bt = jnp.concatenate([jnp.tile(b_out, elem), jnp.zeros((wide - dof,), F32)])[None]
    mask = fixed_mask.reshape(groups, dof).T.astype(F32)
    vm = lambda: pl.BlockSpec(memory_space=pltpu.VMEM)
    sm = lambda: pl.BlockSpec(memory_space=pltpu.SMEM)
    dma = pltpu.SemaphoreType.DMA
    rounds = SWEEPS - 1
    span = n_sy * groups
    n_plane, n_z = 2 * n_sx, n_sy // 2
    needed = (feat + ecoef + 8) * hidden_units // 1024
    per = -(-needed // (2 * n_plane))
    tiles = 2 * n_plane * per
    scratch = [
        pltpu.VMEM((n_rows, hidden_units), F32),
        pltpu.VMEM((n_rows, hidden_units), BF16),
        pltpu.VMEM((feat, n_rows), BF16),
        pltpu.VMEM((groups, wide), F32),
        pltpu.VMEM((groups, wide), F32),
        pltpu.VMEM((n_sy, groups, wide), F32),
        pltpu.VMEM((n_sy, groups, wide), F32),
        pltpu.VMEM((n_sy, groups, wide), F32),
        pltpu.VMEM((span, groups * lanes), BF16),
        pltpu.VMEM((bx, dof, 2 * dof), F32),
        pltpu.VMEM((by, dof, 2 * dof), F32),
        pltpu.VMEM((bx, by, dof, 4 * dof), BF16),
        pltpu.VMEM((bx, by, dof, 3 * dof), BF16),
        pltpu.VMEM((bx, by, dof, 3 * dof), BF16),
        pltpu.VMEM((bx, by, dof, 3 * dof), BF16),
        pltpu.VMEM((bx, by, dof, 3 * dof), BF16),
        pltpu.VMEM((bx, by, dof, lanes), F32),
        pltpu.VMEM((bx, by, dof, lanes), F32),
        pltpu.VMEM((bx, by, dof, lanes), F32),
        pltpu.VMEM((SWEEPS, bx, by, dof, 2 * lanes), F32),
        pltpu.VMEM((rounds, bx, dof, 2 * lanes), F32),
        pltpu.VMEM((rounds, bx, dof, 2 * lanes), F32),
        pltpu.VMEM((rounds, by, dof, 2 * lanes), F32),
        pltpu.VMEM((rounds, by, dof, 2 * lanes), F32),
        pltpu.VMEM((2, bx + 2, by + 2, dof, 2 * lanes), BF16),
        pltpu.VMEM((SWEEPS, bx, by, dof, lanes), F32),
        pltpu.VMEM((bx, by, dof, lanes), F32),
        pltpu.VMEM((bx, by, dof, lanes), F32),
        pltpu.VMEM((dof, groups * lanes), BF16),
        pltpu.VMEM((dof, groups * lanes), BF16),
        pltpu.VMEM((tiles, 8, 128), F32),
        pltpu.VMEM((tiles // 2, 8, 128), F32),
        pltpu.VMEM((tiles // 2, 8, 128), F32),
        pltpu.VMEM((n_plane, per, 8, 128), F32),
        pltpu.VMEM((n_z, per, 8, 128), F32),
        pltpu.VMEM((tiles, 8, 128), F32),
        dma((n_sy,)), dma((n_sy,)), dma((2,)), dma((2,)),
        dma((2, rounds, bx)), dma((2, rounds, bx)), dma((2, rounds)), dma((2, rounds)),
        dma((n_sy,)), dma((n_sy,)),
        dma((2,)), dma((2,)), dma((2, n_plane)), dma((2, n_plane)), dma((n_z,)), dma((n_z,)),
    ]
    field, w_in_grad, b_in_grad, w_out_grad, b_out_grad = pl.pallas_call(
        functools.partial(kernel, n_sx, n_sy),
        out_shape=(
            jax.ShapeDtypeStruct((bx, by, dof, lanes), F32),
            jax.ShapeDtypeStruct((feat, hidden_units), F32),
            jax.ShapeDtypeStruct((1, hidden_units), F32),
            jax.ShapeDtypeStruct((hidden_units, ecoef), F32),
            jax.ShapeDtypeStruct((1, ecoef), F32),
        ),
        in_specs=[vm()] * 8 + [sm(), vm()],
        out_specs=(vm(), vm(), vm(), vm(), vm()),
        scratch_shapes=scratch,
        compiler_params=pltpu.CompilerParams(
            collective_id=0, has_side_effects=True, vmem_limit_bytes=48 * 1024 * 1024
        ),
    )(picked, w_in, b_in[None], wt, bt, block_rows[0], loads[0], mask, elem_map[0], cotangent[0])
    return (field[None], w_in_grad, b_in_grad[0], w_out_grad, b_out_grad[0])


def solution(mesh):
    placed = (
        P("sec", "sx", "sy", None, None, None),
        P("sec", "sx", "sy"),
        P(),
        P(),
        P(),
        P(),
        P("sec", "sx", "sy", None, None),
        P("sec", "sx", "sy", None, None),
        P("sec", "sx", "sy", None),
        P("sec", "sx", "sy"),
        P("sec", "sx", "sy", None, None),
    )
    return jax.shard_map(
        local,
        mesh=mesh,
        in_specs=placed,
        out_specs=(P("sec", "sx", "sy", None, None), P(), P(), P(), P()),
        check_vma=False,
    )
```

```python
import functools

import jax
import jax.numpy as jnp
from jax import lax
from jax.experimental import pallas as pl
from jax.experimental.pallas import tpu as pltpu
from jax.sharding import PartitionSpec as P

SWEEPS = 4
RELAXATION = 0.8
F32 = jnp.float32
BF16 = jnp.bfloat16
MESH = pl.DeviceIdType.MESH


def mm(a, b):
    return jnp.dot(a, b, preferred_element_type=F32)


def mm_nt(a, b):
    return lax.dot_general(a, b, (((1,), (1,)), ((), ())), preferred_element_type=F32)


def split(v):
    hi = v.astype(BF16)
    lo = (v - hi.astype(F32)).astype(BF16)
    return hi, lo


def mul3(m3, v):
    hi, lo = split(v)
    return mm(m3, jnp.concatenate([hi, hi, lo], axis=0))


def put3(ref, bx, by, m):
    d = m.shape[0]
    hi, lo = split(m)
    ref[bx, by, :, 0:d] = hi
    ref[bx, by, :, d : 2 * d] = lo
    ref[bx, by, :, 2 * d : 3 * d] = hi


def kernel(
    n_sx, n_sy, picked_ref, w_in_ref, b_in_ref, wt_ref, b_out_ref, rows_in, loads_in, mask_ref, map_ref,
    cot_in, u_ref, wg_ref, bi_ref, wo_ref, bo_ref,
    pre, hid, pick_t, gate, own, gath, placed, back, oh, kh_w, kh_s, cm, kd3, kdt3, p3, pt3, mw, cw, rc,
    x_st, h_w, h_e, h_s, h_n, xb, tt, ku, gh, acc_hi, acc_lo,
    red, half, got_core, got_plane, got_z, summed, rows_ref, loads_ref, cot_ref, s_in,
    sg, rg, sk, rk, s_we, r_we, s_ns, r_ns, sc, rcs, s_core, r_core, s_plane, r_plane, s_z, r_z,
):
    bx, by, dof = rows_ref.shape[0], rows_ref.shape[1], rows_ref.shape[2]
    groups = bx * by
    lanes = loads_ref.shape[3]
    fetches = [
        pltpu.make_async_copy(src, dst, s_in.at[i])
        for i, (src, dst) in enumerate(((rows_in, rows_ref), (loads_in, loads_ref), (cot_in, cot_ref)))
    ]
    for fetch in fetches:
        fetch.start()
    sec, sx, sy = lax.axis_index("sec"), lax.axis_index("sx"), lax.axis_index("sy")
    has_w, has_e, has_s, has_n = sy > 0, sy < n_sy - 1, sx > 0, sx < n_sx - 1
    west, east = (sec, sx, sy - 1), (sec, sx, sy + 1)
    south, north = (sec, sx - 1, sy), (sec, sx + 1, sy)

    n_plane, n_z = 2 * n_sx, n_sy // 2
    core, my_z, my_plane = lax.rem(sy, 2), sy // 2, sec * n_sx + sx
    mate = (sec, sx, sy + 1 - 2 * core)
    plane_dev = lambda i: (i // n_sx, lax.rem(i, n_sx), sy)
    z_dev = lambda i: (sec, sx, 2 * i + core)

    barrier = pltpu.get_barrier_semaphore()
    pl.semaphore_signal(barrier, inc=1, device_id=mate, device_id_type=MESH)
    for k in range(1, n_plane):
        pl.semaphore_signal(
            barrier, inc=1, device_id=plane_dev(lax.rem(my_plane + k, n_plane)), device_id_type=MESH
        )
    for k in range(1, n_z):
        pl.semaphore_signal(barrier, inc=1, device_id=z_dev(lax.rem(my_z + k, n_z)), device_id_type=MESH)
    for k in range(n_sy):
        pl.semaphore_signal(
            barrier, inc=1, device_id=(1 - sec, sx, lax.rem(sy + k, n_sy)), device_id_type=MESH
        )
    for has, dev in ((has_w, west), (has_e, east), (has_s, south), (has_n, north)):

        @pl.when(has)
        def _():
            pl.semaphore_signal(barrier, inc=1, device_id=dev, device_id_type=MESH)

    pre_in = mm(picked_ref[...], w_in_ref[...]) + b_in_ref[...]
    pre[...] = pre_in
    hidden = (pre_in * jax.nn.sigmoid(pre_in)).astype(BF16)
    hid[...] = hidden
    n_rows = hidden.shape[0]
    full = jax.nn.sigmoid(mm_nt(hidden, wt_ref[...]) + b_out_ref[...])
    elem = n_rows // groups
    width = dof // elem
    wide = full.shape[1]
    row_id = lax.broadcasted_iota(jnp.int32, (n_rows, wide), 0)
    col_id = lax.broadcasted_iota(jnp.int32, (n_rows, wide), 1)
    mine = (row_id % elem) == (col_id // width)
    gate_rows = jnp.sum(jnp.where(mine, full, 0.0).reshape(groups, elem, wide), axis=1)
    gate[...] = gate_rows
    own[...] = 0.5 + 2.0 * gate_rows

    one = lambda has: jnp.where(has, 1, 0)
    pl.semaphore_wait(barrier, n_sy + n_plane + n_z - 1 + one(has_w) + one(has_e) + one(has_s) + one(has_n))

    def group_copy(k):
        j = lax.rem(sy + k, n_sy)
        return pltpu.make_async_remote_copy(
            src_ref=own, dst_ref=gath.at[sy], send_sem=sg.at[k], recv_sem=rg.at[sy],
            device_id=(1 - sec, sx, j), device_id_type=MESH,
        )

    for k in range(n_sy):
        group_copy(k).start()
    for fetch in fetches:
        fetch.wait()

    def kw_copy():
        return pltpu.make_async_remote_copy(
            src_ref=rows_ref.at[:, by - 1, :, pl.ds(0, 2 * dof)], dst_ref=kh_w,
            send_sem=sk.at[0], recv_sem=rk.at[0], device_id=east, device_id_type=MESH,
        )

    def ks_copy():
        return pltpu.make_async_remote_copy(
            src_ref=rows_ref.at[bx - 1, :, :, pl.ds(2 * dof, 2 * dof)], dst_ref=kh_s,
            send_sem=sk.at[1], recv_sem=rk.at[1], device_id=north, device_id_type=MESH,
        )

    @pl.when(has_e)
    def _():
        kw_copy().start()

    @pl.when(has_n)
    def _():
        ks_copy().start()

    zero_block = jnp.zeros((dof, dof), BF16)
    for x in range(bx):
        for y in range(by):
            block = rows_ref[x, y]
            turned = block.T
            cm[x, y, :, 0 : 2 * dof] = block[:, dof : 3 * dof].astype(BF16)
            put3(kd3, x, y, block[:, 0:dof])
            put3(p3, x, y, block[:, 3 * dof : 4 * dof])
            put3(kdt3, x, y, turned[0:dof])
            put3(pt3, x, y, turned[3 * dof : 4 * dof])
            if y + 1 < by:
                cm[x, y + 1, :, 2 * dof : 3 * dof] = turned[dof : 2 * dof].astype(BF16)
            if x + 1 < bx:
                cm[x + 1, y, :, 3 * dof : 4 * dof] = turned[2 * dof : 3 * dof].astype(BF16)
            mw[x, y] = jnp.broadcast_to(mask_ref[:, x * by + y : x * by + y + 1], (dof, lanes))
    pick_t[...] = picked_ref[...].astype(F32).T.astype(BF16)
    xb[...] = jnp.zeros_like(xb)

    span = n_sy * groups
    ids = lax.broadcasted_iota(jnp.int32, (span, lanes), 0)
    gid = (ids // groups) * by + ids % by
    gx = (ids // by) % bx
    for x in range(bx):
        for y in range(by):
            b = x * by + y
            hit = (gid == map_ref[x, y]) & (gx == x)
            oh[:, b * lanes : (b + 1) * lanes] = jnp.where(hit, 1.0, 0.0).astype(BF16)

    for j in range(n_sy):
        pltpu.make_async_remote_copy(
            src_ref=own, dst_ref=gath.at[j], send_sem=sg.at[j], recv_sem=rg.at[j],
            device_id=(1 - sec, sx, j), device_id_type=MESH,
        ).wait_recv()
    turned_rows = gath[...].reshape(span, wide).T[0:dof]
    g_hi, g_lo = split(turned_rows)
    for x in range(bx):
        part = oh[:, x * by * lanes : (x + 1) * by * lanes]
        coefs = mm(g_hi, part) + mm(g_lo, part)
        for y in range(by):
            c = coefs[:, y * lanes : (y + 1) * lanes]
            rc[x, y] = 1.0 / c

    def face(direction, r, x):
        if direction == 0:
            return pltpu.make_async_remote_copy(
                src_ref=x_st.at[r, x, 0], dst_ref=h_e.at[r, x], send_sem=s_we.at[0, r, x],
                recv_sem=r_we.at[0, r, x], device_id=west, device_id_type=MESH,
            )
        if direction == 1:
            return pltpu.make_async_remote_copy(
                src_ref=x_st.at[r, x, by - 1], dst_ref=h_w.at[r, x], send_sem=s_we.at[1, r, x],
                recv_sem=r_we.at[1, r, x], device_id=east, device_id_type=MESH,
            )
        if direction == 2:
            return pltpu.make_async_remote_copy(
                src_ref=x_st.at[r, 0], dst_ref=h_n.at[r], send_sem=s_ns.at[0, r],
                recv_sem=r_ns.at[0, r], device_id=south, device_id_type=MESH,
            )
        return pltpu.make_async_remote_copy(
            src_ref=x_st.at[r, bx - 1], dst_ref=h_s.at[r], send_sem=s_ns.at[1, r],
            recv_sem=r_ns.at[1, r], device_id=north, device_id_type=MESH,
        )

    def send_row(r, x):
        @pl.when((r < SWEEPS - 1) & (x == bx - 1) & has_n)
        def _():
            face(3, r, x).start()

        @pl.when((r < SWEEPS - 1) & (x == 0) & has_s)
        def _():
            face(2, r, x).start()

        @pl.when((r < SWEEPS - 1) & has_w)
        def _():
            face(0, r, x).start()

        @pl.when((r < SWEEPS - 1) & has_e)
        def _():
            face(1, r, x).start()

    step = 2 if bx % 2 == 0 else 1

    def rows_at(k):
        first = k * step
        return [jnp.where(sx == 0, first + i, bx - 1 - first - i) for i in range(step)]

    def cells(rows):
        return [(x, y) for x in rows for y in range(by)]

    def finish(r, at, us, hs):
        ps = [RELAXATION * mul3(pt3[c], h) for c, h in zip(at, hs)]
        ws = [p * rc[c] for c, p in zip(at, ps)]
        slot = lax.rem(r, 2)
        for (x, y), u, h, p, w in zip(at, us, hs, ps, ws):
            x_st[r, x, y, :, 0:lanes] = u
            x_st[r, x, y, :, lanes : 2 * lanes] = w
            xb[slot, x + 1, y + 1, :, 0:lanes] = u.astype(BF16)
            xb[slot, x + 1, y + 1, :, lanes : 2 * lanes] = w.astype(BF16)
            u_ref[x, y] = u
            gh[x, y] = h
            cw[x, y] = p

    def after(at):
        gs = [gh[c] - mul3(kdt3[c], cw[c]) for c in at]
        ks = [mul3(kd3[c], u_ref[c]) for c in at]
        for c, g, k in zip(at, gs, ks):
            gh[c] = g
            ku[c] = k

    def first_rows(k, _):
        rows = rows_at(k)
        at = cells(rows)
        ts = [loads_ref[c].astype(F32) * rc[c] for c in at]
        us = [mw[c] * (RELAXATION * mul3(p3[c], t)) for c, t in zip(at, ts)]
        hs = [mw[c] * cot_ref[c].astype(F32) for c in at]
        finish(0, at, us, hs)
        for c, t in zip(at, ts):
            tt[(0, *c)] = t
        for x in rows:
            send_row(0, x)
        after(at)
        return 0

    lax.fori_loop(0, bx // step, first_rows, 0)

    @pl.when(has_w)
    def _():
        kw_copy().wait_recv()
        for x in range(bx):
            cm[x, 0, :, 2 * dof : 3 * dof] = kh_w[x].T[dof : 2 * dof].astype(BF16)

    @pl.when(jnp.logical_not(has_w))
    def _():
        for x in range(bx):
            cm[x, 0, :, 2 * dof : 3 * dof] = zero_block

    @pl.when(has_s)
    def _():
        ks_copy().wait_recv()
        for y in range(by):
            cm[0, y, :, 3 * dof : 4 * dof] = kh_s[y].T[0:dof].astype(BF16)

    @pl.when(jnp.logical_not(has_s))
    def _():
        for y in range(by):
            cm[0, y, :, 3 * dof : 4 * dof] = zero_block

    def sweep(r, _):
        old = lax.rem(r - 1, 2)

        def sweep_rows(k, _):
            rows = rows_at(k)
            for x in rows:
                @pl.when(has_w)
                def _():
                    face(1, r - 1, x).wait_recv()
                    xb[old, x + 1, 0] = h_w[r - 1, x].astype(BF16)

                @pl.when(has_e)
                def _():
                    face(0, r - 1, x).wait_recv()
                    xb[old, x + 1, by + 1] = h_e[r - 1, x].astype(BF16)

                @pl.when((x == 0) & has_s)
                def _():
                    face(3, r - 1, x).wait_recv()
                    for y in range(by):
                        xb[old, 0, y + 1] = h_s[r - 1, y].astype(BF16)

                @pl.when((x == bx - 1) & has_n)
                def _():
                    face(2, r - 1, x).wait_recv()
                    for y in range(by):
                        xb[old, bx + 1, y + 1] = h_n[r - 1, y].astype(BF16)

            at = cells(rows)
            cs = []
            for x, y in at:
                near = jnp.concatenate(
                    [xb[old, x + 1, y + 2], xb[old, x + 2, y + 1], xb[old, x + 1, y], xb[old, x, y + 1]],
                    axis=0,
                )
                cs.append(mm(cm[x, y], near))
            ts = [(loads_ref[a].astype(F32) - c[:, 0:lanes]) * rc[a] for a, c in zip(at, cs)]
            hs = [mw[a] * (gh[a] - c[:, lanes : 2 * lanes]) for a, c in zip(at, cs)]
            us = [mw[a] * (u_ref[a] + RELAXATION * mul3(p3[a], t - ku[a])) for a, t in zip(at, ts)]
            finish(r, at, us, hs)
            for c, t in zip(at, ts):
                tt[(r, *c)] = t
            for x in rows:
                send_row(r, x)

            @pl.when(r < SWEEPS - 1)
            def _():
                after(at)

            return 0

        return lax.fori_loop(0, bx // step, sweep_rows, 0)

    lax.fori_loop(1, SWEEPS, sweep, 0)

    for x in range(bx):
        for y in range(by):
            total = tt[0, x, y] * x_st[SWEEPS - 1, x, y, :, lanes : 2 * lanes]
            for r in range(1, SWEEPS):
                total = total + tt[r, x, y] * x_st[SWEEPS - 1 - r, x, y, :, lanes : 2 * lanes]
            hi, lo = split(-total)
            b = x * by + y
            acc_hi[:, b * lanes : (b + 1) * lanes] = hi
            acc_lo[:, b * lanes : (b + 1) * lanes] = lo
    sums = mm_nt(oh[...], acc_hi[...]) + mm_nt(oh[...], acc_lo[...])
    sums = jnp.concatenate([sums, jnp.zeros((span, wide - dof), F32)], axis=1)
    placed[...] = sums.reshape(n_sy, groups, wide)

    def grad_copy(k):
        j = lax.rem(sy + k, n_sy)
        return pltpu.make_async_remote_copy(
            src_ref=placed.at[j], dst_ref=back.at[sy], send_sem=sc.at[k], recv_sem=rcs.at[sy],
            device_id=(1 - sec, sx, j), device_id_type=MESH,
        )

    for k in range(n_sy):
        grad_copy(k).start()

    pre_in = pre[...]
    q = jax.nn.sigmoid(pre_in)
    slope = q + pre_in * q * (1.0 - q)

    for j in range(n_sy):
        pltpu.make_async_remote_copy(
            src_ref=placed.at[j], dst_ref=back.at[j], send_sem=sc.at[j], recv_sem=rcs.at[j],
            device_id=(1 - sec, sx, j), device_id_type=MESH,
        ).wait_recv()
    net_grad = jnp.sum(back[...], axis=0)
    g = gate[...]
    out_term = net_grad * (2.0 * g * (1.0 - g))
    spread = jnp.broadcast_to(out_term[:, None, :], (groups, elem, wide)).reshape(n_rows, wide)
    spread = jnp.where(mine, spread, 0.0)
    out_round = spread.astype(BF16)
    turned_out = spread.T.astype(BF16)
    w_out_t = mm(turned_out, hid[...])[0:dof]
    hidden_units = w_out_t.shape[1]
    in_term = mm(out_round, wt_ref[...]) * slope
    w_in_grad = mm(pick_t[...], in_term.astype(BF16))
    extra = jnp.concatenate(
        [
            jnp.sum(w_out_t.reshape(elem, width, hidden_units), axis=0),
            jnp.sum(in_term, axis=0, keepdims=True),
            jnp.concatenate(
                [jnp.sum(out_term, axis=0, keepdims=True), jnp.zeros((1, hidden_units - wide), F32)], axis=1
            ),
            jnp.zeros((6, hidden_units), F32),
        ],
        axis=0,
    )

    feat = w_in_grad.shape[0]
    strips, deep, more = hidden_units // 128, feat // 8, extra.shape[0] // 8
    tiles = red.shape[0]
    n_half, per = tiles // 2, got_z.shape[1]
    used = strips * (deep + more)
    for c in range(strips):
        red[c * deep : (c + 1) * deep] = w_in_grad[:, c * 128 : (c + 1) * 128].reshape(deep, 8, 128)
        at = strips * deep + c * more
        red[at : at + more] = extra[:, c * 128 : (c + 1) * 128].reshape(more, 8, 128)
    if used < tiles:
        red[used:tiles] = jnp.zeros((tiles - used, 8, 128), F32)

    def core_copy(step, src, dst):
        return pltpu.make_async_remote_copy(
            src_ref=src, dst_ref=dst, send_sem=s_core.at[step], recv_sem=r_core.at[step],
            device_id=mate, device_id_type=MESH,
        )

    give = core_copy(0, red.at[pl.ds((1 - core) * n_half, n_half)], got_core)
    give.start()
    give.wait_recv()
    half[...] = red[pl.ds(core * n_half, n_half)] + got_core[...]

    def plane_copy(step, k, src, dst, slot):
        return pltpu.make_async_remote_copy(
            src_ref=src, dst_ref=dst, send_sem=s_plane.at[step, k], recv_sem=r_plane.at[step, slot],
            device_id=plane_dev(lax.rem(my_plane + k, n_plane)), device_id_type=MESH,
        )

    def plane_give(k):
        to = lax.rem(my_plane + k, n_plane)
        return plane_copy(0, k, half.at[pl.ds(to * per, per)], got_plane.at[my_plane], my_plane)

    def plane_got(k):
        source = lax.rem(my_plane + k, n_plane)
        return plane_copy(0, k, half.at[pl.ds(0, per)], got_plane.at[source], source)

    for k in range(1, n_plane):
        plane_give(k).start()
    part = half[pl.ds(my_plane * per, per)]
    for k in range(1, n_plane):
        plane_got(k).wait_recv()
        part = part + got_plane[lax.rem(my_plane + k, n_plane)]
    got_z[my_z] = part

    def z_copy(k, slot):
        return pltpu.make_async_remote_copy(
            src_ref=got_z.at[my_z], dst_ref=got_z.at[slot], send_sem=s_z.at[k], recv_sem=r_z.at[slot],
            device_id=z_dev(lax.rem(my_z + k, n_z)), device_id_type=MESH,
        )

    for k in range(1, n_z):
        z_copy(k, my_z).start()
    for k in range(1, n_z):
        z_copy(k, lax.rem(my_z + k, n_z)).wait_recv()
    base = core * n_half
    mine_at = pl.ds(base + my_plane * per, per)
    summed[mine_at] = jnp.sum(got_z[...], axis=0)

    def plane_spread(k):
        return plane_copy(1, k, summed.at[mine_at], summed.at[mine_at], my_plane)

    def plane_fill(k):
        source = lax.rem(my_plane + k, n_plane)
        there = summed.at[pl.ds(base + source * per, per)]
        return plane_copy(1, k, there, there, source)

    for k in range(1, n_plane):
        plane_spread(k).start()
    for k in range(1, n_plane):
        plane_fill(k).wait_recv()
    spread_half = core_copy(1, summed.at[pl.ds(base, n_half)], summed.at[pl.ds(base, n_half)])
    spread_half.start()
    other = summed.at[pl.ds((1 - core) * n_half, n_half)]
    core_copy(1, other, other).wait_recv()

    sums = []
    for c in range(strips):
        wg_ref[:, c * 128 : (c + 1) * 128] = summed[c * deep : (c + 1) * deep].reshape(feat, 128)
        at = strips * deep + c * more
        piece = summed[at : at + more].reshape(8 * more, 128)
        wo_ref[:, c * 128 : (c + 1) * 128] = piece[0:width]
        bi_ref[:, c * 128 : (c + 1) * 128] = piece[width : width + 1]
        if c == 0:
            folded = piece[width + 1 : width + 2, 0:width]
            for e in range(1, elem):
                folded = folded + piece[width + 1 : width + 2, e * width : (e + 1) * width]
            bo_ref[...] = folded

    give.wait_send()
    spread_half.wait_send()
    for k in range(1, n_plane):
        plane_give(k).wait_send()
        plane_spread(k).wait_send()
    for k in range(1, n_z):
        z_copy(k, my_z).wait_send()
    for k in range(n_sy):
        group_copy(k).wait_send()
        grad_copy(k).wait_send()

    @pl.when(has_e)
    def _():
        kw_copy().wait_send()

    @pl.when(has_n)
    def _():
        ks_copy().wait_send()

    for r in range(SWEEPS - 1):
        for x in range(bx):

            @pl.when(has_w)
            def _():
                face(0, r, x).wait_send()

            @pl.when(has_e)
            def _():
                face(1, r, x).wait_send()

        @pl.when(has_s)
        def _():
            face(2, r, 0).wait_send()

        @pl.when(has_n)
        def _():
            face(3, r, 0).wait_send()


def write_out(*refs):
    sem = refs[-1]
    copies = [pltpu.make_async_copy(refs[i], refs[i + 5], sem.at[i]) for i in range(5)]
    for c in copies:
        c.start()
    for c in copies:
        c.wait()


def local(
    replay, replay_pick, w_in, b_in, w_out, b_out, block_rows, loads, fixed_mask, elem_map, cotangent
):
    _, bx, by, dof, _ = block_rows.shape
    lanes = loads.shape[-1]
    n_sx, n_sy = lax.axis_size("sx"), lax.axis_size("sy")
    feat, hidden_units = w_in.shape
    ecoef = w_out.shape[1]
    groups = bx * by
    wide = 2 * dof
    picked = replay[:, :, :, 0]
    picked = jnp.where((replay_pick == 1)[..., None, None], replay[:, :, :, 1], picked)
    picked = picked.reshape(-1, feat)
    n_rows = picked.shape[0]
    elem = n_rows // groups
    wt = jnp.concatenate([jnp.tile(w_out.T, (elem, 1)), jnp.zeros((wide - dof, hidden_units), BF16)], axis=0)
    bt = jnp.concatenate([jnp.tile(b_out, elem), jnp.zeros((wide - dof,), F32)])[None]
    mask = fixed_mask.reshape(groups, dof).T.astype(F32)
    vm = lambda: pl.BlockSpec(memory_space=pltpu.VMEM)
    hbm = lambda: pl.BlockSpec(memory_space=pl.ANY)
    sm = lambda: pl.BlockSpec(memory_space=pltpu.SMEM)
    dma = pltpu.SemaphoreType.DMA
    rounds = SWEEPS - 1
    span = n_sy * groups
    n_plane, n_z = 2 * n_sx, n_sy // 2
    needed = (feat + ecoef + 8) * hidden_units // 1024
    per = -(-needed // (2 * n_plane))
    tiles = 2 * n_plane * per
    scratch = [
        pltpu.VMEM((n_rows, hidden_units), F32),
        pltpu.VMEM((n_rows, hidden_units), BF16),
        pltpu.VMEM((feat, n_rows), BF16),
        pltpu.VMEM((groups, wide), F32),
        pltpu.VMEM((groups, wide), F32),
        pltpu.VMEM((n_sy, groups, wide), F32),
        pltpu.VMEM((n_sy, groups, wide), F32),
        pltpu.VMEM((n_sy, groups, wide), F32),
        pltpu.VMEM((span, groups * lanes), BF16),
        pltpu.VMEM((bx, dof, 2 * dof), F32),
        pltpu.VMEM((by, dof, 2 * dof), F32),
        pltpu.VMEM((bx, by, dof, 4 * dof), BF16),
        pltpu.VMEM((bx, by, dof, 3 * dof), BF16),
        pltpu.VMEM((bx, by, dof, 3 * dof), BF16),
        pltpu.VMEM((bx, by, dof, 3 * dof), BF16),
        pltpu.VMEM((bx, by, dof, 3 * dof), BF16),
        pltpu.VMEM((bx, by, dof, lanes), F32),
        pltpu.VMEM((bx, by, dof, lanes), F32),
        pltpu.VMEM((bx, by, dof, lanes), F32),
        pltpu.VMEM((SWEEPS, bx, by, dof, 2 * lanes), F32),
        pltpu.VMEM((rounds, bx, dof, 2 * lanes), F32),
        pltpu.VMEM((rounds, bx, dof, 2 * lanes), F32),
        pltpu.VMEM((rounds, by, dof, 2 * lanes), F32),
        pltpu.VMEM((rounds, by, dof, 2 * lanes), F32),
        pltpu.VMEM((2, bx + 2, by + 2, dof, 2 * lanes), BF16),
        pltpu.VMEM((SWEEPS, bx, by, dof, lanes), F32),
        pltpu.VMEM((bx, by, dof, lanes), F32),
        pltpu.VMEM((bx, by, dof, lanes), F32),
        pltpu.VMEM((dof, groups * lanes), BF16),
        pltpu.VMEM((dof, groups * lanes), BF16),
        pltpu.VMEM((tiles, 8, 128), F32),
        pltpu.VMEM((tiles // 2, 8, 128), F32),
        pltpu.VMEM((tiles // 2, 8, 128), F32),
        pltpu.VMEM((n_plane, per, 8, 128), F32),
        pltpu.VMEM((n_z, per, 8, 128), F32),
        pltpu.VMEM((tiles, 8, 128), F32),
        pltpu.VMEM(block_rows.shape[1:], F32),
        pltpu.VMEM(loads.shape[1:], BF16),
        pltpu.VMEM(cotangent.shape[1:], BF16),
        dma((3,)),
        dma((n_sy,)), dma((n_sy,)), dma((2,)), dma((2,)),
        dma((2, rounds, bx)), dma((2, rounds, bx)), dma((2, rounds)), dma((2, rounds)),
        dma((n_sy,)), dma((n_sy,)),
        dma((2,)), dma((2,)), dma((2, n_plane)), dma((2, n_plane)), dma((n_z,)), dma((n_z,)),
    ]
    results = pl.pallas_call(
        functools.partial(kernel, n_sx, n_sy),
        out_shape=(
            jax.ShapeDtypeStruct((bx, by, dof, lanes), F32),
            jax.ShapeDtypeStruct((feat, hidden_units), F32),
            jax.ShapeDtypeStruct((1, hidden_units), F32),
            jax.ShapeDtypeStruct((ecoef, hidden_units), F32),
            jax.ShapeDtypeStruct((1, ecoef), F32),
        ),
        in_specs=[vm()] * 5 + [hbm(), hbm(), vm(), sm(), hbm()],
        out_specs=(vm(), vm(), vm(), vm(), vm()),
        scratch_shapes=scratch,
        compiler_params=pltpu.CompilerParams(
            collective_id=0, has_side_effects=True, vmem_limit_bytes=56 * 1024 * 1024
        ),
    )(picked, w_in, b_in[None], wt, bt, block_rows[0], loads[0], mask, elem_map[0], cotangent[0])
    field, w_in_grad, b_in_grad, w_out_grad, b_out_grad = pl.pallas_call(
        write_out,
        out_shape=tuple(jax.ShapeDtypeStruct(r.shape, r.dtype) for r in results),
        in_specs=[hbm()] * 5,
        out_specs=(hbm(),) * 5,
        scratch_shapes=[dma((5,))],
    )(*results)
    return (field[None], w_in_grad, b_in_grad[0], w_out_grad.T, b_out_grad[0])


def solution(mesh):
    placed = (
        P("sec", "sx", "sy", None, None, None),
        P("sec", "sx", "sy"),
        P(),
        P(),
        P(),
        P(),
        P("sec", "sx", "sy", None, None),
        P("sec", "sx", "sy", None, None),
        P("sec", "sx", "sy", None),
        P("sec", "sx", "sy"),
        P("sec", "sx", "sy", None, None),
    )
    return jax.shard_map(
        local,
        mesh=mesh,
        in_specs=placed,
        out_specs=(P("sec", "sx", "sy", None, None), P(), P(), P(), P()),
        check_vma=False,
    )
```

```python
import functools

import jax
import jax.numpy as jnp
from jax import lax
from jax.experimental import pallas as pl
from jax.experimental.pallas import tpu as pltpu
from jax.sharding import PartitionSpec as P

SWEEPS = 4
RELAXATION = 0.8
F32 = jnp.float32
BF16 = jnp.bfloat16
MESH = pl.DeviceIdType.MESH


def mm(a, b):
    return jnp.dot(a, b, preferred_element_type=F32)


def mm_nt(a, b):
    return lax.dot_general(a, b, (((1,), (1,)), ((), ())), preferred_element_type=F32)


def split(v):
    hi = v.astype(BF16)
    lo = (v - hi.astype(F32)).astype(BF16)
    return hi, lo


def mul3(m3, v):
    hi, lo = split(v)
    return mm(m3, jnp.concatenate([hi, hi, lo], axis=0))


def put3(ref, bx, by, m):
    d = m.shape[0]
    hi, lo = split(m)
    ref[bx, by, :, 0:d] = hi
    ref[bx, by, :, d : 2 * d] = lo
    ref[bx, by, :, 2 * d : 3 * d] = hi


def kernel(
    n_sx, n_sy, picked_ref, w_in_ref, b_in_ref, wt_ref, b_out_ref, rows_in, loads_in, mask_ref, map_ref,
    cot_in, u_ref, wg_ref, bi_ref, wo_ref, bo_ref,
    pre, hid, pick_t, gate, own, gath, placed, back, oh, kh_w, kh_s, cm, kd3, kdt3, p3, pt3, mw, cw, rc,
    x_st, h_w, h_e, h_s, h_n, xb, tt, ku, gh, acc_hi, acc_lo,
    red, half, got_core, got_plane, got_z, summed, rows_ref, loads_ref, cot_ref, s_in,
    sg, rg, sk, rk, s_we, r_we, s_ns, r_ns, sc, rcs, s_core, r_core, s_plane, r_plane, s_z, r_z,
):
    bx, by, dof = rows_ref.shape[0], rows_ref.shape[1], rows_ref.shape[2]
    groups = bx * by
    lanes = loads_ref.shape[3]
    fetches = [
        pltpu.make_async_copy(src, dst, s_in.at[i])
        for i, (src, dst) in enumerate(((rows_in, rows_ref), (loads_in, loads_ref), (cot_in, cot_ref)))
    ]
    for fetch in fetches:
        fetch.start()
    sec, sx, sy = lax.axis_index("sec"), lax.axis_index("sx"), lax.axis_index("sy")
    has_w, has_e, has_s, has_n = sy > 0, sy < n_sy - 1, sx > 0, sx < n_sx - 1
    west, east = (sec, sx, sy - 1), (sec, sx, sy + 1)
    south, north = (sec, sx - 1, sy), (sec, sx + 1, sy)

    n_plane, n_z = 2 * n_sx, n_sy // 2
    core, my_z, my_plane = lax.rem(sy, 2), sy // 2, sec * n_sx + sx
    mate = (sec, sx, sy + 1 - 2 * core)
    plane_dev = lambda i: (i // n_sx, lax.rem(i, n_sx), sy)
    z_dev = lambda i: (sec, sx, 2 * i + core)

    barrier = pltpu.get_barrier_semaphore()
    pl.semaphore_signal(barrier, inc=1, device_id=mate, device_id_type=MESH)
    for k in range(1, n_plane):
        pl.semaphore_signal(
            barrier, inc=1, device_id=plane_dev(lax.rem(my_plane + k, n_plane)), device_id_type=MESH
        )
    for k in range(1, n_z):
        pl.semaphore_signal(barrier, inc=1, device_id=z_dev(lax.rem(my_z + k, n_z)), device_id_type=MESH)
    for k in range(n_sy):
        pl.semaphore_signal(
            barrier, inc=1, device_id=(1 - sec, sx, lax.rem(sy + k, n_sy)), device_id_type=MESH
        )
    for has, dev in ((has_w, west), (has_e, east), (has_s, south), (has_n, north)):

        @pl.when(has)
        def _():
            pl.semaphore_signal(barrier, inc=1, device_id=dev, device_id_type=MESH)

    pre_in = mm(picked_ref[...], w_in_ref[...]) + b_in_ref[...]
    pre[...] = pre_in
    hidden = (pre_in * jax.nn.sigmoid(pre_in)).astype(BF16)
    hid[...] = hidden
    n_rows = hidden.shape[0]
    full = jax.nn.sigmoid(mm_nt(hidden, wt_ref[...]) + b_out_ref[...])
    elem = n_rows // groups
    width = dof // elem
    wide = full.shape[1]
    row_id = lax.broadcasted_iota(jnp.int32, (n_rows, wide), 0)
    col_id = lax.broadcasted_iota(jnp.int32, (n_rows, wide), 1)
    mine = (row_id % elem) == (col_id // width)
    gate_rows = jnp.sum(jnp.where(mine, full, 0.0).reshape(groups, elem, wide), axis=1)
    gate[...] = gate_rows
    own[...] = 0.5 + 2.0 * gate_rows

    one = lambda has: jnp.where(has, 1, 0)
    pl.semaphore_wait(barrier, n_sy + n_plane + n_z - 1 + one(has_w) + one(has_e) + one(has_s) + one(has_n))

    def group_copy(k):
        j = lax.rem(sy + k, n_sy)
        return pltpu.make_async_remote_copy(
            src_ref=own, dst_ref=gath.at[sy], send_sem=sg.at[k], recv_sem=rg.at[sy],
            device_id=(1 - sec, sx, j), device_id_type=MESH,
        )

    for k in range(n_sy):
        group_copy(k).start()
    for fetch in fetches:
        fetch.wait()

    def kw_copy():
        return pltpu.make_async_remote_copy(
            src_ref=rows_ref.at[:, by - 1, :, pl.ds(0, 2 * dof)], dst_ref=kh_w,
            send_sem=sk.at[0], recv_sem=rk.at[0], device_id=east, device_id_type=MESH,
        )

    def ks_copy():
        return pltpu.make_async_remote_copy(
            src_ref=rows_ref.at[bx - 1, :, :, pl.ds(2 * dof, 2 * dof)], dst_ref=kh_s,
            send_sem=sk.at[1], recv_sem=rk.at[1], device_id=north, device_id_type=MESH,
        )

    @pl.when(has_e)
    def _():
        kw_copy().start()

    @pl.when(has_n)
    def _():
        ks_copy().start()

    zero_block = jnp.zeros((dof, dof), BF16)
    for x in range(bx):
        for y in range(by):
            block = rows_ref[x, y]
            turned = block.T
            cm[x, y, :, 0 : 2 * dof] = block[:, dof : 3 * dof].astype(BF16)
            put3(kd3, x, y, block[:, 0:dof])
            put3(p3, x, y, block[:, 3 * dof : 4 * dof])
            put3(kdt3, x, y, turned[0:dof])
            put3(pt3, x, y, turned[3 * dof : 4 * dof])
            if y + 1 < by:
                cm[x, y + 1, :, 2 * dof : 3 * dof] = turned[dof : 2 * dof].astype(BF16)
            if x + 1 < bx:
                cm[x + 1, y, :, 3 * dof : 4 * dof] = turned[2 * dof : 3 * dof].astype(BF16)
            mw[x, y] = jnp.broadcast_to(mask_ref[:, x * by + y : x * by + y + 1], (dof, lanes))
    pick_t[...] = picked_ref[...].astype(F32).T.astype(BF16)
    xb[...] = jnp.zeros_like(xb)

    span = n_sy * groups
    ids = lax.broadcasted_iota(jnp.int32, (span, lanes), 0)
    gid = (ids // groups) * by + ids % by
    gx = (ids // by) % bx
    for x in range(bx):
        for y in range(by):
            b = x * by + y
            hit = (gid == map_ref[x, y]) & (gx == x)
            oh[:, b * lanes : (b + 1) * lanes] = jnp.where(hit, 1.0, 0.0).astype(BF16)

    for j in range(n_sy):
        pltpu.make_async_remote_copy(
            src_ref=own, dst_ref=gath.at[j], send_sem=sg.at[j], recv_sem=rg.at[j],
            device_id=(1 - sec, sx, j), device_id_type=MESH,
        ).wait_recv()
    turned_rows = gath[...].reshape(span, wide).T[0:dof]
    g_hi, g_lo = split(turned_rows)
    for x in range(bx):
        part = oh[:, x * by * lanes : (x + 1) * by * lanes]
        coefs = mm(g_hi, part) + mm(g_lo, part)
        for y in range(by):
            c = coefs[:, y * lanes : (y + 1) * lanes]
            rc[x, y] = 1.0 / c

    def face(direction, r, x):
        if direction == 0:
            return pltpu.make_async_remote_copy(
                src_ref=x_st.at[r, x, 0], dst_ref=h_e.at[r, x], send_sem=s_we.at[0, r, x],
                recv_sem=r_we.at[0, r, x], device_id=west, device_id_type=MESH,
            )
        if direction == 1:
            return pltpu.make_async_remote_copy(
                src_ref=x_st.at[r, x, by - 1], dst_ref=h_w.at[r, x], send_sem=s_we.at[1, r, x],
                recv_sem=r_we.at[1, r, x], device_id=east, device_id_type=MESH,
            )
        if direction == 2:
            return pltpu.make_async_remote_copy(
                src_ref=x_st.at[r, 0], dst_ref=h_n.at[r], send_sem=s_ns.at[0, r],
                recv_sem=r_ns.at[0, r], device_id=south, device_id_type=MESH,
            )
        return pltpu.make_async_remote_copy(
            src_ref=x_st.at[r, bx - 1], dst_ref=h_s.at[r], send_sem=s_ns.at[1, r],
            recv_sem=r_ns.at[1, r], device_id=north, device_id_type=MESH,
        )

    def send_row(r, x):
        @pl.when((r < SWEEPS - 1) & (x == bx - 1) & has_n)
        def _():
            face(3, r, x).start()

        @pl.when((r < SWEEPS - 1) & (x == 0) & has_s)
        def _():
            face(2, r, x).start()

        @pl.when((r < SWEEPS - 1) & has_w)
        def _():
            face(0, r, x).start()

        @pl.when((r < SWEEPS - 1) & has_e)
        def _():
            face(1, r, x).start()

    step = 2 if bx % 2 == 0 else 1

    def rows_at(k):
        first = k * step
        return [jnp.where(sx == 0, first + i, bx - 1 - first - i) for i in range(step)]

    def cells(rows):
        return [(x, y) for x in rows for y in range(by)]

    def finish(r, at, us, hs):
        ps = [RELAXATION * mul3(pt3[c], h) for c, h in zip(at, hs)]
        ws = [p * rc[c] for c, p in zip(at, ps)]
        slot = lax.rem(r, 2)
        for (x, y), u, h, p, w in zip(at, us, hs, ps, ws):
            x_st[r, x, y, :, 0:lanes] = u
            x_st[r, x, y, :, lanes : 2 * lanes] = w
            xb[slot, x + 1, y + 1, :, 0:lanes] = u.astype(BF16)
            xb[slot, x + 1, y + 1, :, lanes : 2 * lanes] = w.astype(BF16)
            u_ref[x, y] = u
            gh[x, y] = h
            cw[x, y] = p

    def after(at):
        gs = [gh[c] - mul3(kdt3[c], cw[c]) for c in at]
        ks = [mul3(kd3[c], u_ref[c]) for c in at]
        for c, g, k in zip(at, gs, ks):
            gh[c] = g
            ku[c] = k

    def first_rows(k, _):
        rows = rows_at(k)
        at = cells(rows)
        ts = [loads_ref[c].astype(F32) * rc[c] for c in at]
        us = [mw[c] * (RELAXATION * mul3(p3[c], t)) for c, t in zip(at, ts)]
        hs = [mw[c] * cot_ref[c].astype(F32) for c in at]
        finish(0, at, us, hs)
        for c, t in zip(at, ts):
            tt[(0, *c)] = t
        for x in rows:
            send_row(0, x)
        after(at)
        return 0

    lax.fori_loop(0, bx // step, first_rows, 0)

    @pl.when(has_w)
    def _():
        kw_copy().wait_recv()
        for x in range(bx):
            cm[x, 0, :, 2 * dof : 3 * dof] = kh_w[x].T[dof : 2 * dof].astype(BF16)

    @pl.when(jnp.logical_not(has_w))
    def _():
        for x in range(bx):
            cm[x, 0, :, 2 * dof : 3 * dof] = zero_block

    @pl.when(has_s)
    def _():
        ks_copy().wait_recv()
        for y in range(by):
            cm[0, y, :, 3 * dof : 4 * dof] = kh_s[y].T[0:dof].astype(BF16)

    @pl.when(jnp.logical_not(has_s))
    def _():
        for y in range(by):
            cm[0, y, :, 3 * dof : 4 * dof] = zero_block

    def sweep(r, _):
        old = lax.rem(r - 1, 2)

        def sweep_rows(k, _):
            rows = rows_at(k)
            for x in rows:
                @pl.when(has_w)
                def _():
                    face(1, r - 1, x).wait_recv()
                    xb[old, x + 1, 0] = h_w[r - 1, x].astype(BF16)

                @pl.when(has_e)
                def _():
                    face(0, r - 1, x).wait_recv()
                    xb[old, x + 1, by + 1] = h_e[r - 1, x].astype(BF16)

                @pl.when((x == 0) & has_s)
                def _():
                    face(3, r - 1, x).wait_recv()
                    for y in range(by):
                        xb[old, 0, y + 1] = h_s[r - 1, y].astype(BF16)

                @pl.when((x == bx - 1) & has_n)
                def _():
                    face(2, r - 1, x).wait_recv()
                    for y in range(by):
                        xb[old, bx + 1, y + 1] = h_n[r - 1, y].astype(BF16)

            at = cells(rows)
            cs = []
            for x, y in at:
                near = jnp.concatenate(
                    [xb[old, x + 1, y + 2], xb[old, x + 2, y + 1], xb[old, x + 1, y], xb[old, x, y + 1]],
                    axis=0,
                )
                cs.append(mm(cm[x, y], near))
            ts = [(loads_ref[a].astype(F32) - c[:, 0:lanes]) * rc[a] for a, c in zip(at, cs)]
            hs = [mw[a] * (gh[a] - c[:, lanes : 2 * lanes]) for a, c in zip(at, cs)]
            us = [mw[a] * (u_ref[a] + RELAXATION * mul3(p3[a], t - ku[a])) for a, t in zip(at, ts)]
            finish(r, at, us, hs)
            for c, t in zip(at, ts):
                tt[(r, *c)] = t
            for x in rows:
                send_row(r, x)

            @pl.when(r < SWEEPS - 1)
            def _():
                after(at)

            return 0

        return lax.fori_loop(0, bx // step, sweep_rows, 0)

    lax.fori_loop(1, SWEEPS, sweep, 0)

    for x in range(bx):
        for y in range(by):
            total = tt[0, x, y] * x_st[SWEEPS - 1, x, y, :, lanes : 2 * lanes]
            for r in range(1, SWEEPS):
                total = total + tt[r, x, y] * x_st[SWEEPS - 1 - r, x, y, :, lanes : 2 * lanes]
            hi, lo = split(-total)
            b = x * by + y
            acc_hi[:, b * lanes : (b + 1) * lanes] = hi
            acc_lo[:, b * lanes : (b + 1) * lanes] = lo
    sums = mm_nt(oh[...], acc_hi[...]) + mm_nt(oh[...], acc_lo[...])
    sums = jnp.concatenate([sums, jnp.zeros((span, wide - dof), F32)], axis=1)
    placed[...] = sums.reshape(n_sy, groups, wide)

    def grad_copy(k):
        j = lax.rem(sy + k, n_sy)
        return pltpu.make_async_remote_copy(
            src_ref=placed.at[j], dst_ref=back.at[sy], send_sem=sc.at[k], recv_sem=rcs.at[sy],
            device_id=(1 - sec, sx, j), device_id_type=MESH,
        )

    for k in range(n_sy):
        grad_copy(k).start()

    pre_in = pre[...]
    q = jax.nn.sigmoid(pre_in)
    slope = q + pre_in * q * (1.0 - q)

    for j in range(n_sy):
        pltpu.make_async_remote_copy(
            src_ref=placed.at[j], dst_ref=back.at[j], send_sem=sc.at[j], recv_sem=rcs.at[j],
            device_id=(1 - sec, sx, j), device_id_type=MESH,
        ).wait_recv()
    net_grad = jnp.sum(back[...], axis=0)
    g = gate[...]
    out_term = net_grad * (2.0 * g * (1.0 - g))
    spread = jnp.broadcast_to(out_term[:, None, :], (groups, elem, wide)).reshape(n_rows, wide)
    spread = jnp.where(mine, spread, 0.0)
    out_round = spread.astype(BF16)
    turned_out = spread.T.astype(BF16)
    w_out_t = mm(turned_out, hid[...])[0:dof]
    hidden_units = w_out_t.shape[1]
    in_term = mm(out_round, wt_ref[...]) * slope
    w_in_grad = mm(pick_t[...], in_term.astype(BF16))
    extra = jnp.concatenate(
        [
            jnp.sum(w_out_t.reshape(elem, width, hidden_units), axis=0),
            jnp.sum(in_term, axis=0, keepdims=True),
            jnp.concatenate(
                [jnp.sum(out_term, axis=0, keepdims=True), jnp.zeros((1, hidden_units - wide), F32)], axis=1
            ),
            jnp.zeros((6, hidden_units), F32),
        ],
        axis=0,
    )

    feat = w_in_grad.shape[0]
    strips, deep, more = hidden_units // 128, feat // 8, extra.shape[0] // 8
    tiles = red.shape[0]
    n_half, per = tiles // 2, got_z.shape[1]
    used = strips * (deep + more)
    for c in range(strips):
        red[c * deep : (c + 1) * deep] = w_in_grad[:, c * 128 : (c + 1) * 128].reshape(deep, 8, 128)
        at = strips * deep + c * more
        red[at : at + more] = extra[:, c * 128 : (c + 1) * 128].reshape(more, 8, 128)
    if used < tiles:
        red[used:tiles] = jnp.zeros((tiles - used, 8, 128), F32)

    def core_copy(step, src, dst):
        return pltpu.make_async_remote_copy(
            src_ref=src, dst_ref=dst, send_sem=s_core.at[step], recv_sem=r_core.at[step],
            device_id=mate, device_id_type=MESH,
        )

    give = core_copy(0, red.at[pl.ds((1 - core) * n_half, n_half)], got_core)
    give.start()
    give.wait_recv()
    half[...] = red[pl.ds(core * n_half, n_half)] + got_core[...]

    def plane_copy(step, k, src, dst, slot):
        return pltpu.make_async_remote_copy(
            src_ref=src, dst_ref=dst, send_sem=s_plane.at[step, k], recv_sem=r_plane.at[step, slot],
            device_id=plane_dev(lax.rem(my_plane + k, n_plane)), device_id_type=MESH,
        )

    def plane_give(k):
        to = lax.rem(my_plane + k, n_plane)
        return plane_copy(0, k, half.at[pl.ds(to * per, per)], got_plane.at[my_plane], my_plane)

    def plane_got(k):
        source = lax.rem(my_plane + k, n_plane)
        return plane_copy(0, k, half.at[pl.ds(0, per)], got_plane.at[source], source)

    for k in range(1, n_plane):
        plane_give(k).start()
    part = half[pl.ds(my_plane * per, per)]
    for k in range(1, n_plane):
        plane_got(k).wait_recv()
        part = part + got_plane[lax.rem(my_plane + k, n_plane)]
    got_z[my_z] = part

    def z_copy(k, slot):
        return pltpu.make_async_remote_copy(
            src_ref=got_z.at[my_z], dst_ref=got_z.at[slot], send_sem=s_z.at[k], recv_sem=r_z.at[slot],
            device_id=z_dev(lax.rem(my_z + k, n_z)), device_id_type=MESH,
        )

    for k in range(1, n_z):
        z_copy(k, my_z).start()
    for k in range(1, n_z):
        z_copy(k, lax.rem(my_z + k, n_z)).wait_recv()
    base = core * n_half
    mine_at = pl.ds(base + my_plane * per, per)
    summed[mine_at] = jnp.sum(got_z[...], axis=0)

    def plane_spread(k):
        return plane_copy(1, k, summed.at[mine_at], summed.at[mine_at], my_plane)

    def plane_fill(k):
        source = lax.rem(my_plane + k, n_plane)
        there = summed.at[pl.ds(base + source * per, per)]
        return plane_copy(1, k, there, there, source)

    for k in range(1, n_plane):
        plane_spread(k).start()
    for k in range(1, n_plane):
        plane_fill(k).wait_recv()
    spread_half = core_copy(1, summed.at[pl.ds(base, n_half)], summed.at[pl.ds(base, n_half)])
    spread_half.start()
    other = summed.at[pl.ds((1 - core) * n_half, n_half)]
    core_copy(1, other, other).wait_recv()

    sums = []
    for c in range(strips):
        wg_ref[:, c * 128 : (c + 1) * 128] = summed[c * deep : (c + 1) * deep].reshape(feat, 128)
        at = strips * deep + c * more
        piece = summed[at : at + more].reshape(8 * more, 128)
        wo_ref[:, c * 128 : (c + 1) * 128] = piece[0:width]
        bi_ref[:, c * 128 : (c + 1) * 128] = piece[width : width + 1]
        if c == 0:
            folded = piece[width + 1 : width + 2, 0:width]
            for e in range(1, elem):
                folded = folded + piece[width + 1 : width + 2, e * width : (e + 1) * width]
            bo_ref[...] = folded

    give.wait_send()
    spread_half.wait_send()
    for k in range(1, n_plane):
        plane_give(k).wait_send()
        plane_spread(k).wait_send()
    for k in range(1, n_z):
        z_copy(k, my_z).wait_send()
    for k in range(n_sy):
        group_copy(k).wait_send()
        grad_copy(k).wait_send()

    @pl.when(has_e)
    def _():
        kw_copy().wait_send()

    @pl.when(has_n)
    def _():
        ks_copy().wait_send()

    for r in range(SWEEPS - 1):
        for x in range(bx):

            @pl.when(has_w)
            def _():
                face(0, r, x).wait_send()

            @pl.when(has_e)
            def _():
                face(1, r, x).wait_send()

        @pl.when(has_s)
        def _():
            face(2, r, 0).wait_send()

        @pl.when(has_n)
        def _():
            face(3, r, 0).wait_send()


def write_out(*refs):
    sem = refs[-1]
    copies = [pltpu.make_async_copy(refs[i], refs[i + 5], sem.at[i]) for i in range(5)]
    for c in copies:
        c.start()
    for c in copies:
        c.wait()


def local(
    replay, replay_pick, w_in, b_in, w_out, b_out, block_rows, loads, fixed_mask, elem_map, cotangent
):
    _, bx, by, dof, _ = block_rows.shape
    lanes = loads.shape[-1]
    n_sx, n_sy = lax.axis_size("sx"), lax.axis_size("sy")
    feat, hidden_units = w_in.shape
    ecoef = w_out.shape[1]
    groups = bx * by
    wide = 2 * dof
    picked = replay[:, :, :, 0]
    picked = jnp.where((replay_pick == 1)[..., None, None], replay[:, :, :, 1], picked)
    picked = picked.reshape(-1, feat)
    n_rows = picked.shape[0]
    elem = n_rows // groups
    wt = jnp.concatenate([jnp.tile(w_out.T, (elem, 1)), jnp.zeros((wide - dof, hidden_units), BF16)], axis=0)
    bt = jnp.concatenate([jnp.tile(b_out, elem), jnp.zeros((wide - dof,), F32)])[None]
    mask = fixed_mask.reshape(groups, dof).T.astype(F32)
    vm = lambda: pl.BlockSpec(memory_space=pltpu.VMEM)
    hbm = lambda: pl.BlockSpec(memory_space=pl.ANY)
    sm = lambda: pl.BlockSpec(memory_space=pltpu.SMEM)
    dma = pltpu.SemaphoreType.DMA
    rounds = SWEEPS - 1
    span = n_sy * groups
    n_plane, n_z = 2 * n_sx, n_sy // 2
    needed = (feat + ecoef + 8) * hidden_units // 1024
    per = -(-needed // (2 * n_plane))
    tiles = 2 * n_plane * per
    scratch = [
        pltpu.VMEM((n_rows, hidden_units), F32),
        pltpu.VMEM((n_rows, hidden_units), BF16),
        pltpu.VMEM((feat, n_rows), BF16),
        pltpu.VMEM((groups, wide), F32),
        pltpu.VMEM((groups, wide), F32),
        pltpu.VMEM((n_sy, groups, wide), F32),
        pltpu.VMEM((n_sy, groups, wide), F32),
        pltpu.VMEM((n_sy, groups, wide), F32),
        pltpu.VMEM((span, groups * lanes), BF16),
        pltpu.VMEM((bx, dof, 2 * dof), F32),
        pltpu.VMEM((by, dof, 2 * dof), F32),
        pltpu.VMEM((bx, by, dof, 4 * dof), BF16),
        pltpu.VMEM((bx, by, dof, 3 * dof), BF16),
        pltpu.VMEM((bx, by, dof, 3 * dof), BF16),
        pltpu.VMEM((bx, by, dof, 3 * dof), BF16),
        pltpu.VMEM((bx, by, dof, 3 * dof), BF16),
        pltpu.VMEM((bx, by, dof, lanes), F32),
        pltpu.VMEM((bx, by, dof, lanes), F32),
        pltpu.VMEM((bx, by, dof, lanes), F32),
        pltpu.VMEM((SWEEPS, bx, by, dof, 2 * lanes), F32),
        pltpu.VMEM((rounds, bx, dof, 2 * lanes), F32),
        pltpu.VMEM((rounds, bx, dof, 2 * lanes), F32),
        pltpu.VMEM((rounds, by, dof, 2 * lanes), F32),
        pltpu.VMEM((rounds, by, dof, 2 * lanes), F32),
        pltpu.VMEM((2, bx + 2, by + 2, dof, 2 * lanes), BF16),
        pltpu.VMEM((SWEEPS, bx, by, dof, lanes), F32),
        pltpu.VMEM((bx, by, dof, lanes), F32),
        pltpu.VMEM((bx, by, dof, lanes), F32),
        pltpu.VMEM((dof, groups * lanes), BF16),
        pltpu.VMEM((dof, groups * lanes), BF16),
        pltpu.VMEM((tiles, 8, 128), F32),
        pltpu.VMEM((tiles // 2, 8, 128), F32),
        pltpu.VMEM((tiles // 2, 8, 128), F32),
        pltpu.VMEM((n_plane, per, 8, 128), F32),
        pltpu.VMEM((n_z, per, 8, 128), F32),
        pltpu.VMEM((tiles, 8, 128), F32),
        pltpu.VMEM(block_rows.shape[1:], F32),
        pltpu.VMEM(loads.shape[1:], BF16),
        pltpu.VMEM(cotangent.shape[1:], BF16),
        dma((3,)),
        dma((n_sy,)), dma((n_sy,)), dma((2,)), dma((2,)),
        dma((2, rounds, bx)), dma((2, rounds, bx)), dma((2, rounds)), dma((2, rounds)),
        dma((n_sy,)), dma((n_sy,)),
        dma((2,)), dma((2,)), dma((2, n_plane)), dma((2, n_plane)), dma((n_z,)), dma((n_z,)),
    ]
    results = pl.pallas_call(
        functools.partial(kernel, n_sx, n_sy),
        out_shape=(
            jax.ShapeDtypeStruct((bx, by, dof, lanes), F32),
            jax.ShapeDtypeStruct((feat, hidden_units), F32),
            jax.ShapeDtypeStruct((1, hidden_units), F32),
            jax.ShapeDtypeStruct((ecoef, hidden_units), F32),
            jax.ShapeDtypeStruct((1, ecoef), F32),
        ),
        in_specs=[vm()] * 5 + [hbm(), hbm(), vm(), sm(), hbm()],
        out_specs=(vm(), vm(), vm(), vm(), vm()),
        scratch_shapes=scratch,
        compiler_params=pltpu.CompilerParams(
            collective_id=0, has_side_effects=True, vmem_limit_bytes=40 * 1024 * 1024
        ),
    )(picked, w_in, b_in[None], wt, bt, block_rows[0], loads[0], mask, elem_map[0], cotangent[0])
    field, w_in_grad, b_in_grad, w_out_grad, b_out_grad = pl.pallas_call(
        write_out,
        out_shape=tuple(jax.ShapeDtypeStruct(r.shape, r.dtype) for r in results),
        in_specs=[vm()] * 5,
        out_specs=(hbm(),) * 5,
        scratch_shapes=[dma((5,))],
    )(*results)
    return (field[None], w_in_grad, b_in_grad[0], w_out_grad.T, b_out_grad[0])


def solution(mesh):
    placed = (
        P("sec", "sx", "sy", None, None, None),
        P("sec", "sx", "sy"),
        P(),
        P(),
        P(),
        P(),
        P("sec", "sx", "sy", None, None),
        P("sec", "sx", "sy", None, None),
        P("sec", "sx", "sy", None),
        P("sec", "sx", "sy"),
        P("sec", "sx", "sy", None, None),
    )
    return jax.shard_map(
        local,
        mesh=mesh,
        in_specs=placed,
        out_specs=(P("sec", "sx", "sy", None, None), P(), P(), P(), P()),
        check_vma=False,
    )
```

```python
import functools

import jax
import jax.numpy as jnp
from jax import lax
from jax.experimental import pallas as pl
from jax.experimental.pallas import tpu as pltpu
from jax.sharding import PartitionSpec as P

SWEEPS = 4
RELAXATION = 0.8
F32 = jnp.float32
BF16 = jnp.bfloat16
MESH = pl.DeviceIdType.MESH


def mm(a, b):
    return jnp.dot(a, b, preferred_element_type=F32)


def mm_nt(a, b):
    return lax.dot_general(a, b, (((1,), (1,)), ((), ())), preferred_element_type=F32)


def split(v):
    hi = v.astype(BF16)
    lo = (v - hi.astype(F32)).astype(BF16)
    return hi, lo


def mul3(m3, v):
    hi, lo = split(v)
    return mm(m3, jnp.concatenate([hi, hi, lo], axis=0))


def put3(ref, bx, by, m):
    d = m.shape[0]
    hi, lo = split(m)
    ref[bx, by, :, 0:d] = hi
    ref[bx, by, :, d : 2 * d] = lo
    ref[bx, by, :, 2 * d : 3 * d] = hi


def kernel(
    n_sx, n_sy, picked_ref, w_in_ref, b_in_ref, wt_ref, b_out_ref, rows_in, loads_in, mask_ref, map_ref,
    cot_in, u_ref, wg_ref, bi_ref, wo_ref, bo_ref,
    pre, hid, pick_t, gate, own, gath, placed, back, oh, kh_w, kh_s, cm, kd3, kdt3, p3, pt3, mw, cw, rc,
    x_st, h_w, h_e, h_s, h_n, xb, tt, ku, gh, acc_hi, acc_lo,
    red, half, got_core, got_plane, got_z, summed, rows_ref, loads_ref, cot_ref, s_in,
    sg, rg, sk, rk, s_we, r_we, s_ns, r_ns, sc, rcs, s_core, r_core, s_plane, r_plane, s_z, r_z,
):
    bx, by, dof = rows_ref.shape[0], rows_ref.shape[1], rows_ref.shape[2]
    groups = bx * by
    lanes = loads_ref.shape[3]
    fetches = [
        pltpu.make_async_copy(src, dst, s_in.at[i])
        for i, (src, dst) in enumerate(((rows_in, rows_ref), (loads_in, loads_ref), (cot_in, cot_ref)))
    ]
    for fetch in fetches:
        fetch.start()
    sec, sx, sy = lax.axis_index("sec"), lax.axis_index("sx"), lax.axis_index("sy")
    has_w, has_e, has_s, has_n = sy > 0, sy < n_sy - 1, sx > 0, sx < n_sx - 1
    west, east = (sec, sx, sy - 1), (sec, sx, sy + 1)
    south, north = (sec, sx - 1, sy), (sec, sx + 1, sy)

    n_plane, n_z = 2 * n_sx, n_sy // 2
    core, my_z, my_plane = lax.rem(sy, 2), sy // 2, sec * n_sx + sx
    mate = (sec, sx, sy + 1 - 2 * core)
    plane_dev = lambda i: (i // n_sx, lax.rem(i, n_sx), sy)
    z_dev = lambda i: (sec, sx, 2 * i + core)

    barrier = pltpu.get_barrier_semaphore()
    pl.semaphore_signal(barrier, inc=1, device_id=mate, device_id_type=MESH)
    for k in range(1, n_plane):
        pl.semaphore_signal(
            barrier, inc=1, device_id=plane_dev(lax.rem(my_plane + k, n_plane)), device_id_type=MESH
        )
    for k in range(1, n_z):
        pl.semaphore_signal(barrier, inc=1, device_id=z_dev(lax.rem(my_z + k, n_z)), device_id_type=MESH)
    for k in range(n_sy):
        pl.semaphore_signal(
            barrier, inc=1, device_id=(1 - sec, sx, lax.rem(sy + k, n_sy)), device_id_type=MESH
        )
    for has, dev in ((has_w, west), (has_e, east), (has_s, south), (has_n, north)):

        @pl.when(has)
        def _():
            pl.semaphore_signal(barrier, inc=1, device_id=dev, device_id_type=MESH)

    pre_in = mm(picked_ref[...], w_in_ref[...]) + b_in_ref[...]
    pre[...] = pre_in
    hidden = (pre_in * jax.nn.sigmoid(pre_in)).astype(BF16)
    hid[...] = hidden
    n_rows = hidden.shape[0]
    full = jax.nn.sigmoid(mm_nt(hidden, wt_ref[...]) + b_out_ref[...])
    elem = n_rows // groups
    width = dof // elem
    wide = full.shape[1]
    row_id = lax.broadcasted_iota(jnp.int32, (n_rows, wide), 0)
    col_id = lax.broadcasted_iota(jnp.int32, (n_rows, wide), 1)
    mine = (row_id % elem) == (col_id // width)
    gate_rows = jnp.sum(jnp.where(mine, full, 0.0).reshape(groups, elem, wide), axis=1)
    gate[...] = gate_rows
    own[...] = 0.5 + 2.0 * gate_rows

    one = lambda has: jnp.where(has, 1, 0)
    pl.semaphore_wait(barrier, n_sy + n_plane + n_z - 1 + one(has_w) + one(has_e) + one(has_s) + one(has_n))

    def group_copy(k):
        j = lax.rem(sy + k, n_sy)
        return pltpu.make_async_remote_copy(
            src_ref=own, dst_ref=gath.at[sy], send_sem=sg.at[k], recv_sem=rg.at[sy],
            device_id=(1 - sec, sx, j), device_id_type=MESH,
        )

    for k in range(n_sy):
        group_copy(k).start()
    for fetch in fetches:
        fetch.wait()

    def kw_copy():
        return pltpu.make_async_remote_copy(
            src_ref=rows_ref.at[:, by - 1, :, pl.ds(0, 2 * dof)], dst_ref=kh_w,
            send_sem=sk.at[0], recv_sem=rk.at[0], device_id=east, device_id_type=MESH,
        )

    def ks_copy():
        return pltpu.make_async_remote_copy(
            src_ref=rows_ref.at[bx - 1, :, :, pl.ds(2 * dof, 2 * dof)], dst_ref=kh_s,
            send_sem=sk.at[1], recv_sem=rk.at[1], device_id=north, device_id_type=MESH,
        )

    @pl.when(has_e)
    def _():
        kw_copy().start()

    @pl.when(has_n)
    def _():
        ks_copy().start()

    zero_block = jnp.zeros((dof, dof), BF16)
    for x in range(bx):
        for y in range(by):
            block = rows_ref[x, y]
            turned = block.T
            cm[x, y, :, 0 : 2 * dof] = block[:, dof : 3 * dof].astype(BF16)
            put3(kd3, x, y, block[:, 0:dof])
            put3(p3, x, y, block[:, 3 * dof : 4 * dof])
            put3(kdt3, x, y, turned[0:dof])
            put3(pt3, x, y, turned[3 * dof : 4 * dof])
            if y + 1 < by:
                cm[x, y + 1, :, 2 * dof : 3 * dof] = turned[dof : 2 * dof].astype(BF16)
            if x + 1 < bx:
                cm[x + 1, y, :, 3 * dof : 4 * dof] = turned[2 * dof : 3 * dof].astype(BF16)
            mw[x, y] = jnp.broadcast_to(mask_ref[:, x * by + y : x * by + y + 1], (dof, lanes))
    pick_t[...] = picked_ref[...].astype(F32).T.astype(BF16)
    xb[...] = jnp.zeros_like(xb)

    span = n_sy * groups
    ids = lax.broadcasted_iota(jnp.int32, (span, lanes), 0)
    gid = (ids // groups) * by + ids % by
    gx = (ids // by) % bx
    for x in range(bx):
        for y in range(by):
            b = x * by + y
            hit = (gid == map_ref[x, y]) & (gx == x)
            oh[:, b * lanes : (b + 1) * lanes] = jnp.where(hit, 1.0, 0.0).astype(BF16)

    for j in range(n_sy):
        pltpu.make_async_remote_copy(
            src_ref=own, dst_ref=gath.at[j], send_sem=sg.at[j], recv_sem=rg.at[j],
            device_id=(1 - sec, sx, j), device_id_type=MESH,
        ).wait_recv()
    turned_rows = gath[...].reshape(span, wide).T[0:dof]
    g_hi, g_lo = split(turned_rows)
    for x in range(bx):
        part = oh[:, x * by * lanes : (x + 1) * by * lanes]
        coefs = mm(g_hi, part) + mm(g_lo, part)
        for y in range(by):
            c = coefs[:, y * lanes : (y + 1) * lanes]
            rc[x, y] = 1.0 / c

    def face(direction, r, x):
        if direction == 0:
            return pltpu.make_async_remote_copy(
                src_ref=x_st.at[r, x, 0], dst_ref=h_e.at[r, x], send_sem=s_we.at[0, r, x],
                recv_sem=r_we.at[0, r, x], device_id=west, device_id_type=MESH,
            )
        if direction == 1:
            return pltpu.make_async_remote_copy(
                src_ref=x_st.at[r, x, by - 1], dst_ref=h_w.at[r, x], send_sem=s_we.at[1, r, x],
                recv_sem=r_we.at[1, r, x], device_id=east, device_id_type=MESH,
            )
        if direction == 2:
            return pltpu.make_async_remote_copy(
                src_ref=x_st.at[r, 0], dst_ref=h_n.at[r], send_sem=s_ns.at[0, r],
                recv_sem=r_ns.at[0, r], device_id=south, device_id_type=MESH,
            )
        return pltpu.make_async_remote_copy(
            src_ref=x_st.at[r, bx - 1], dst_ref=h_s.at[r], send_sem=s_ns.at[1, r],
            recv_sem=r_ns.at[1, r], device_id=north, device_id_type=MESH,
        )

    def send_row(r, x):
        @pl.when((r < SWEEPS - 1) & (x == bx - 1) & has_n)
        def _():
            face(3, r, x).start()

        @pl.when((r < SWEEPS - 1) & (x == 0) & has_s)
        def _():
            face(2, r, x).start()

        @pl.when((r < SWEEPS - 1) & has_w)
        def _():
            face(0, r, x).start()

        @pl.when((r < SWEEPS - 1) & has_e)
        def _():
            face(1, r, x).start()

    step = 2 if bx % 2 == 0 else 1

    def rows_at(k):
        first = k * step
        return [jnp.where(sx == 0, first + i, bx - 1 - first - i) for i in range(step)]

    def cells(rows):
        return [(x, y) for x in rows for y in range(by)]

    def finish(r, at, us, hs):
        ps = [RELAXATION * mul3(pt3[c], h) for c, h in zip(at, hs)]
        ws = [p * rc[c] for c, p in zip(at, ps)]
        slot = lax.rem(r, 2)
        for (x, y), u, h, p, w in zip(at, us, hs, ps, ws):
            x_st[r, x, y, :, 0:lanes] = u
            x_st[r, x, y, :, lanes : 2 * lanes] = w
            xb[slot, x + 1, y + 1, :, 0:lanes] = u.astype(BF16)
            xb[slot, x + 1, y + 1, :, lanes : 2 * lanes] = w.astype(BF16)
            u_ref[x, y] = u
            gh[x, y] = h
            cw[x, y] = p

    def after(at):
        gs = [gh[c] - mul3(kdt3[c], cw[c]) for c in at]
        ks = [mul3(kd3[c], u_ref[c]) for c in at]
        for c, g, k in zip(at, gs, ks):
            gh[c] = g
            ku[c] = k

    def first_rows(k, _):
        rows = rows_at(k)
        at = cells(rows)
        ts = [loads_ref[c].astype(F32) * rc[c] for c in at]
        us = [mw[c] * (RELAXATION * mul3(p3[c], t)) for c, t in zip(at, ts)]
        hs = [mw[c] * cot_ref[c].astype(F32) for c in at]
        finish(0, at, us, hs)
        for c, t in zip(at, ts):
            tt[(0, *c)] = t
        for x in rows:
            send_row(0, x)
        after(at)
        return 0

    lax.fori_loop(0, bx // step, first_rows, 0)

    @pl.when(has_w)
    def _():
        kw_copy().wait_recv()
        for x in range(bx):
            cm[x, 0, :, 2 * dof : 3 * dof] = kh_w[x].T[dof : 2 * dof].astype(BF16)

    @pl.when(jnp.logical_not(has_w))
    def _():
        for x in range(bx):
            cm[x, 0, :, 2 * dof : 3 * dof] = zero_block

    @pl.when(has_s)
    def _():
        ks_copy().wait_recv()
        for y in range(by):
            cm[0, y, :, 3 * dof : 4 * dof] = kh_s[y].T[0:dof].astype(BF16)

    @pl.when(jnp.logical_not(has_s))
    def _():
        for y in range(by):
            cm[0, y, :, 3 * dof : 4 * dof] = zero_block

    def sweep(r, _):
        old = lax.rem(r - 1, 2)

        def sweep_rows(k, _):
            rows = rows_at(k)
            for x in rows:
                @pl.when(has_w)
                def _():
                    face(1, r - 1, x).wait_recv()
                    xb[old, x + 1, 0] = h_w[r - 1, x].astype(BF16)

                @pl.when(has_e)
                def _():
                    face(0, r - 1, x).wait_recv()
                    xb[old, x + 1, by + 1] = h_e[r - 1, x].astype(BF16)

                @pl.when((x == 0) & has_s)
                def _():
                    face(3, r - 1, x).wait_recv()
                    for y in range(by):
                        xb[old, 0, y + 1] = h_s[r - 1, y].astype(BF16)

                @pl.when((x == bx - 1) & has_n)
                def _():
                    face(2, r - 1, x).wait_recv()
                    for y in range(by):
                        xb[old, bx + 1, y + 1] = h_n[r - 1, y].astype(BF16)

            at = cells(rows)
            cs = []
            for x, y in at:
                near = jnp.concatenate(
                    [xb[old, x + 1, y + 2], xb[old, x + 2, y + 1], xb[old, x + 1, y], xb[old, x, y + 1]],
                    axis=0,
                )
                cs.append(mm(cm[x, y], near))
            ts = [(loads_ref[a].astype(F32) - c[:, 0:lanes]) * rc[a] for a, c in zip(at, cs)]
            hs = [mw[a] * (gh[a] - c[:, lanes : 2 * lanes]) for a, c in zip(at, cs)]
            us = [mw[a] * (u_ref[a] + RELAXATION * mul3(p3[a], t - ku[a])) for a, t in zip(at, ts)]
            finish(r, at, us, hs)
            for c, t in zip(at, ts):
                tt[(r, *c)] = t
            for x in rows:
                send_row(r, x)

            @pl.when(r < SWEEPS - 1)
            def _():
                after(at)

            return 0

        return lax.fori_loop(0, bx // step, sweep_rows, 0)

    lax.fori_loop(1, SWEEPS, sweep, 0)

    for x in range(bx):
        for y in range(by):
            total = tt[0, x, y] * x_st[SWEEPS - 1, x, y, :, lanes : 2 * lanes]
            for r in range(1, SWEEPS):
                total = total + tt[r, x, y] * x_st[SWEEPS - 1 - r, x, y, :, lanes : 2 * lanes]
            hi, lo = split(-total)
            b = x * by + y
            acc_hi[:, b * lanes : (b + 1) * lanes] = hi
            acc_lo[:, b * lanes : (b + 1) * lanes] = lo
    sums = mm_nt(oh[...], acc_hi[...]) + mm_nt(oh[...], acc_lo[...])
    sums = jnp.concatenate([sums, jnp.zeros((span, wide - dof), F32)], axis=1)
    placed[...] = sums.reshape(n_sy, groups, wide)

    def grad_copy(k):
        j = lax.rem(sy + k, n_sy)
        return pltpu.make_async_remote_copy(
            src_ref=placed.at[j], dst_ref=back.at[sy], send_sem=sc.at[k], recv_sem=rcs.at[sy],
            device_id=(1 - sec, sx, j), device_id_type=MESH,
        )

    for k in range(n_sy):
        grad_copy(k).start()

    pre_in = pre[...]
    q = jax.nn.sigmoid(pre_in)
    slope = q + pre_in * q * (1.0 - q)

    for j in range(n_sy):
        pltpu.make_async_remote_copy(
            src_ref=placed.at[j], dst_ref=back.at[j], send_sem=sc.at[j], recv_sem=rcs.at[j],
            device_id=(1 - sec, sx, j), device_id_type=MESH,
        ).wait_recv()
    net_grad = jnp.sum(back[...], axis=0)
    g = gate[...]
    out_term = net_grad * (2.0 * g * (1.0 - g))
    spread = jnp.broadcast_to(out_term[:, None, :], (groups, elem, wide)).reshape(n_rows, wide)
    spread = jnp.where(mine, spread, 0.0)
    out_round = spread.astype(BF16)
    turned_out = spread.T.astype(BF16)
    w_out_t = mm(turned_out, hid[...])[0:dof]
    hidden_units = w_out_t.shape[1]
    in_term = mm(out_round, wt_ref[...]) * slope
    w_in_grad = mm(pick_t[...], in_term.astype(BF16))
    extra = jnp.concatenate(
        [
            jnp.sum(w_out_t.reshape(elem, width, hidden_units), axis=0),
            jnp.sum(in_term, axis=0, keepdims=True),
            jnp.concatenate(
                [jnp.sum(out_term, axis=0, keepdims=True), jnp.zeros((1, hidden_units - wide), F32)], axis=1
            ),
            jnp.zeros((6, hidden_units), F32),
        ],
        axis=0,
    )

    feat = w_in_grad.shape[0]
    strips, deep, more = hidden_units // 128, feat // 8, extra.shape[0] // 8
    tiles = red.shape[0]
    n_half, per = tiles // 2, got_z.shape[1]
    used = strips * (deep + more)
    for c in range(strips):
        red[c * deep : (c + 1) * deep] = w_in_grad[:, c * 128 : (c + 1) * 128].reshape(deep, 8, 128)
        at = strips * deep + c * more
        red[at : at + more] = extra[:, c * 128 : (c + 1) * 128].reshape(more, 8, 128)
    if used < tiles:
        red[used:tiles] = jnp.zeros((tiles - used, 8, 128), F32)

    def core_copy(step, src, dst):
        return pltpu.make_async_remote_copy(
            src_ref=src, dst_ref=dst, send_sem=s_core.at[step], recv_sem=r_core.at[step],
            device_id=mate, device_id_type=MESH,
        )

    give = core_copy(0, red.at[pl.ds((1 - core) * n_half, n_half)], got_core)
    give.start()
    give.wait_recv()
    half[...] = red[pl.ds(core * n_half, n_half)] + got_core[...]

    def plane_copy(step, k, src, dst, slot):
        return pltpu.make_async_remote_copy(
            src_ref=src, dst_ref=dst, send_sem=s_plane.at[step, k], recv_sem=r_plane.at[step, slot],
            device_id=plane_dev(lax.rem(my_plane + k, n_plane)), device_id_type=MESH,
        )

    def plane_give(k):
        to = lax.rem(my_plane + k, n_plane)
        return plane_copy(0, k, half.at[pl.ds(to * per, per)], got_plane.at[my_plane], my_plane)

    def plane_got(k):
        source = lax.rem(my_plane + k, n_plane)
        return plane_copy(0, k, half.at[pl.ds(0, per)], got_plane.at[source], source)

    for k in range(1, n_plane):
        plane_give(k).start()
    part = half[pl.ds(my_plane * per, per)]
    for k in range(1, n_plane):
        plane_got(k).wait_recv()
        part = part + got_plane[lax.rem(my_plane + k, n_plane)]
    got_z[my_z] = part

    def z_copy(k, slot):
        return pltpu.make_async_remote_copy(
            src_ref=got_z.at[my_z], dst_ref=got_z.at[slot], send_sem=s_z.at[k], recv_sem=r_z.at[slot],
            device_id=z_dev(lax.rem(my_z + k, n_z)), device_id_type=MESH,
        )

    for k in range(1, n_z):
        z_copy(k, my_z).start()
    for k in range(1, n_z):
        z_copy(k, lax.rem(my_z + k, n_z)).wait_recv()
    base = core * n_half
    mine_at = pl.ds(base + my_plane * per, per)
    summed[mine_at] = jnp.sum(got_z[...], axis=0)

    def plane_spread(k):
        return plane_copy(1, k, summed.at[mine_at], summed.at[mine_at], my_plane)

    def plane_fill(k):
        source = lax.rem(my_plane + k, n_plane)
        there = summed.at[pl.ds(base + source * per, per)]
        return plane_copy(1, k, there, there, source)

    for k in range(1, n_plane):
        plane_spread(k).start()
    for k in range(1, n_plane):
        plane_fill(k).wait_recv()
    spread_half = core_copy(1, summed.at[pl.ds(base, n_half)], summed.at[pl.ds(base, n_half)])
    spread_half.start()
    other = summed.at[pl.ds((1 - core) * n_half, n_half)]
    core_copy(1, other, other).wait_recv()

    sums = []
    for c in range(strips):
        wg_ref[:, c * 128 : (c + 1) * 128] = summed[c * deep : (c + 1) * deep].reshape(feat, 128)
        at = strips * deep + c * more
        piece = summed[at : at + more].reshape(8 * more, 128)
        wo_ref[:, c * 128 : (c + 1) * 128] = piece[0:width]
        bi_ref[:, c * 128 : (c + 1) * 128] = piece[width : width + 1]
        if c == 0:
            folded = piece[width + 1 : width + 2, 0:width]
            for e in range(1, elem):
                folded = folded + piece[width + 1 : width + 2, e * width : (e + 1) * width]
            bo_ref[...] = folded

    give.wait_send()
    spread_half.wait_send()
    for k in range(1, n_plane):
        plane_give(k).wait_send()
        plane_spread(k).wait_send()
    for k in range(1, n_z):
        z_copy(k, my_z).wait_send()
    for k in range(n_sy):
        group_copy(k).wait_send()
        grad_copy(k).wait_send()

    @pl.when(has_e)
    def _():
        kw_copy().wait_send()

    @pl.when(has_n)
    def _():
        ks_copy().wait_send()

    for r in range(SWEEPS - 1):
        for x in range(bx):

            @pl.when(has_w)
            def _():
                face(0, r, x).wait_send()

            @pl.when(has_e)
            def _():
                face(1, r, x).wait_send()

        @pl.when(has_s)
        def _():
            face(2, r, 0).wait_send()

        @pl.when(has_n)
        def _():
            face(3, r, 0).wait_send()


def local(
    replay, replay_pick, w_in, b_in, w_out, b_out, block_rows, loads, fixed_mask, elem_map, cotangent
):
    _, bx, by, dof, _ = block_rows.shape
    lanes = loads.shape[-1]
    n_sx, n_sy = lax.axis_size("sx"), lax.axis_size("sy")
    feat, hidden_units = w_in.shape
    ecoef = w_out.shape[1]
    groups = bx * by
    wide = 2 * dof
    picked = replay[:, :, :, 0]
    picked = jnp.where((replay_pick == 1)[..., None, None], replay[:, :, :, 1], picked)
    picked = picked.reshape(-1, feat)
    n_rows = picked.shape[0]
    elem = n_rows // groups
    wt = jnp.concatenate([jnp.tile(w_out.T, (elem, 1)), jnp.zeros((wide - dof, hidden_units), BF16)], axis=0)
    bt = jnp.concatenate([jnp.tile(b_out, elem), jnp.zeros((wide - dof,), F32)])[None]
    mask = fixed_mask.reshape(groups, dof).T.astype(F32)
    vm = lambda: pl.BlockSpec(memory_space=pltpu.VMEM)
    hbm = lambda: pl.BlockSpec(memory_space=pl.ANY)
    sm = lambda: pl.BlockSpec(memory_space=pltpu.SMEM)
    dma = pltpu.SemaphoreType.DMA
    rounds = SWEEPS - 1
    span = n_sy * groups
    n_plane, n_z = 2 * n_sx, n_sy // 2
    needed = (feat + ecoef + 8) * hidden_units // 1024
    per = -(-needed // (2 * n_plane))
    tiles = 2 * n_plane * per
    scratch = [
        pltpu.VMEM((n_rows, hidden_units), F32),
        pltpu.VMEM((n_rows, hidden_units), BF16),
        pltpu.VMEM((feat, n_rows), BF16),
        pltpu.VMEM((groups, wide), F32),
        pltpu.VMEM((groups, wide), F32),
        pltpu.VMEM((n_sy, groups, wide), F32),
        pltpu.VMEM((n_sy, groups, wide), F32),
        pltpu.VMEM((n_sy, groups, wide), F32),
        pltpu.VMEM((span, groups * lanes), BF16),
        pltpu.VMEM((bx, dof, 2 * dof), F32),
        pltpu.VMEM((by, dof, 2 * dof), F32),
        pltpu.VMEM((bx, by, dof, 4 * dof), BF16),
        pltpu.VMEM((bx, by, dof, 3 * dof), BF16),
        pltpu.VMEM((bx, by, dof, 3 * dof), BF16),
        pltpu.VMEM((bx, by, dof, 3 * dof), BF16),
        pltpu.VMEM((bx, by, dof, 3 * dof), BF16),
        pltpu.VMEM((bx, by, dof, lanes), F32),
        pltpu.VMEM((bx, by, dof, lanes), F32),
        pltpu.VMEM((bx, by, dof, lanes), F32),
        pltpu.VMEM((SWEEPS, bx, by, dof, 2 * lanes), F32),
        pltpu.VMEM((rounds, bx, dof, 2 * lanes), F32),
        pltpu.VMEM((rounds, bx, dof, 2 * lanes), F32),
        pltpu.VMEM((rounds, by, dof, 2 * lanes), F32),
        pltpu.VMEM((rounds, by, dof, 2 * lanes), F32),
        pltpu.VMEM((2, bx + 2, by + 2, dof, 2 * lanes), BF16),
        pltpu.VMEM((SWEEPS, bx, by, dof, lanes), F32),
        pltpu.VMEM((bx, by, dof, lanes), F32),
        pltpu.VMEM((bx, by, dof, lanes), F32),
        pltpu.VMEM((dof, groups * lanes), BF16),
        pltpu.VMEM((dof, groups * lanes), BF16),
        pltpu.VMEM((tiles, 8, 128), F32),
        pltpu.VMEM((tiles // 2, 8, 128), F32),
        pltpu.VMEM((tiles // 2, 8, 128), F32),
        pltpu.VMEM((n_plane, per, 8, 128), F32),
        pltpu.VMEM((n_z, per, 8, 128), F32),
        pltpu.VMEM((tiles, 8, 128), F32),
        pltpu.VMEM(block_rows.shape[1:], F32),
        pltpu.VMEM(loads.shape[1:], BF16),
        pltpu.VMEM(cotangent.shape[1:], BF16),
        dma((3,)),
        dma((n_sy,)), dma((n_sy,)), dma((2,)), dma((2,)),
        dma((2, rounds, bx)), dma((2, rounds, bx)), dma((2, rounds)), dma((2, rounds)),
        dma((n_sy,)), dma((n_sy,)),
        dma((2,)), dma((2,)), dma((2, n_plane)), dma((2, n_plane)), dma((n_z,)), dma((n_z,)),
    ]
    results = pl.pallas_call(
        functools.partial(kernel, n_sx, n_sy),
        out_shape=(
            jax.ShapeDtypeStruct((bx, by, dof, lanes), F32),
            jax.ShapeDtypeStruct((feat, hidden_units), F32),
            jax.ShapeDtypeStruct((1, hidden_units), F32),
            jax.ShapeDtypeStruct((ecoef, hidden_units), F32),
            jax.ShapeDtypeStruct((1, ecoef), F32),
        ),
        in_specs=[vm()] * 5 + [hbm(), hbm(), vm(), sm(), hbm()],
        out_specs=(vm(), vm(), vm(), vm(), vm()),
        scratch_shapes=scratch,
        compiler_params=pltpu.CompilerParams(
            collective_id=0, has_side_effects=True, vmem_limit_bytes=40 * 1024 * 1024
        ),
    )(picked, w_in, b_in[None], wt, bt, block_rows[0], loads[0], mask, elem_map[0], cotangent[0])
    field, w_in_grad, b_in_grad, w_out_grad, b_out_grad = results
    return (field[None], w_in_grad, b_in_grad[0], w_out_grad.T, b_out_grad[0])


def solution(mesh):
    placed = (
        P("sec", "sx", "sy", None, None, None),
        P("sec", "sx", "sy"),
        P(),
        P(),
        P(),
        P(),
        P("sec", "sx", "sy", None, None),
        P("sec", "sx", "sy", None, None),
        P("sec", "sx", "sy", None),
        P("sec", "sx", "sy"),
        P("sec", "sx", "sy", None, None),
    )
    return jax.shard_map(
        local,
        mesh=mesh,
        in_specs=placed,
        out_specs=(P("sec", "sx", "sy", None, None), P(), P(), P(), P()),
        check_vma=False,
    )
```
